128 devices in a mesh: bx: 16 (over x, z), by: 8 (over y, core).
Axes of the slice: x: 4, y: 4, z: 4, core: 2. Of those that a mesh axis runs over, the one named last changes fastest.
Arguments:
- tokens: bfloat16 [16, 8, 1024, 512], P('bx', 'by'), may hold values from -6 to 6
- norm_gain: float32 [512], replicated, may hold values from 0.1 to 1.9
- w_query_key: bfloat16 [512, 1024], replicated
- w_value: bfloat16 [512, 512], replicated, may hold values from -1 to 1
- w_out: bfloat16 [512, 512], replicated, may hold values from -0.25 to 0.25
- cotangent: bfloat16 [16, 8, 1024, 512], P('bx', 'by'), may hold values from -6 to 6
- block_order: int32 [16, 8, 1024], P('bx', 'by'), may hold values from 0 to 1023, each once within a row
- neighbour_ids: int32 [16, 8, 4, 4], replicated, may hold values from 0 to 511, as said below
- neighbour_count: int32 [16, 8, 4], replicated, may hold values from 1 to 4
Outputs:
- branch_out: bfloat16 [16, 8, 1024, 512], P('bx', 'by')
- grad_tokens: float32 [16, 8, 1024, 512], P('bx', 'by')
- grad_w_query_key: float32 [512, 1024], replicated
- grad_w_value: float32 [512, 512], replicated
- grad_w_out: float32 [512, 512], replicated
- grad_norm_gain: float32 [512], replicated
The draws below stay inside these ranges and needn't reach their ends.
Inputs may be any that keep to these rules, and one draw needn't show every extreme that they name: `neighbour_ids`: block ids are (x * 8 + y) * 4 + b. Entry j < neighbour_count of query block b on brick (x, y) names a block other than b itself, either another block of brick (x, y) or a block of a brick one step away along exactly one axis (x - 1, x + 1, y - 1 or y + 1); the live entries of one list differ. Entries from neighbour_count on hold the query block's own id. Over all query blocks of one brick, at most 2 distinct blocks of any one other brick are named, and every brick names exactly 2 blocks of some other brick. `block_order`: on every brick, a permutation of the arrival rows.
All inputs are finite; a program needn't handle non-finite values.
Results may differ from the reference program's by a relative error of at most 0.006.
The reference program's roundings to bfloat16 on the way count: a program that leaves them out, or rounds other values in their place, can miss the bound.
Values may be sent and summed in bfloat16 or wider, within the bound.
No kernel may reach another device: no remote copies, remote signals or barrier semaphores. Data moves between devices by JAX's collectives and lax.ppermute only.
A program may use at most 256 MiB of HBM per device.

```python
import math
import jax
import jax.numpy as jnp
from jax import lax

D = 512
HEADS = 8
BLK = 256
NB = 4
CAP = 2
BLK_DEV = 4
TOK_DEV = 1024
BRICKS_X = 16
BRICKS_Y = 8


def neighbour_tables(key):
    base_key = jax.random.fold_in(key, 7)
    key_offer, key_score, key_first, key_second = jax.random.split(base_key, 4)
    grid_x = jnp.arange(BRICKS_X, dtype=jnp.int32)[:, None, None]
    grid_y = jnp.arange(BRICKS_Y, dtype=jnp.int32)[None, :, None]
    step_x = jnp.array([-1, 1, 0, 0], dtype=jnp.int32)
    step_y = jnp.array([0, 0, -1, 1], dtype=jnp.int32)
    near_x, near_y = jnp.broadcast_arrays(grid_x + step_x, grid_y + step_y)
    inside = (near_x >= 0) & (near_x < BRICKS_X) & (near_y >= 0) & (near_y < BRICKS_Y)
    near_brick = jnp.clip(near_x, 0, BRICKS_X - 1) * BRICKS_Y + jnp.clip(near_y, 0, BRICKS_Y - 1)
    block_range = jnp.arange(BLK_DEV, dtype=jnp.int32)
    offer_scores = jax.random.randint(key_offer, (BRICKS_X, BRICKS_Y, 4, BLK_DEV), 0, 1 << 20) * BLK_DEV + block_range
    offered = jnp.argsort(offer_scores, axis=-1, stable=True)[..., :CAP].astype(jnp.int32)
    offer_ids = (near_brick[..., None] * BLK_DEV + offered).reshape(BRICKS_X, BRICKS_Y, 4 * CAP)
    offer_fine = jnp.repeat(inside, CAP, axis=-1)
    own_brick = grid_x[..., 0] * BRICKS_Y + grid_y[..., 0]
    own_ids = own_brick[..., None] * BLK_DEV + block_range
    columns = BLK_DEV + 4 * CAP
    candidates = jnp.concatenate([jnp.broadcast_to(own_ids[:, :, None, :], (BRICKS_X, BRICKS_Y, BLK_DEV, BLK_DEV)), jnp.broadcast_to(offer_ids[:, :, None, :], (BRICKS_X, BRICKS_Y, BLK_DEV, 4 * CAP))], axis=-1)
    candidate_fine = jnp.concatenate([jnp.broadcast_to(block_range[:, None] != block_range[None, :], (BRICKS_X, BRICKS_Y, BLK_DEV, BLK_DEV)), jnp.broadcast_to(offer_fine[:, :, None, :], (BRICKS_X, BRICKS_Y, BLK_DEV, 4 * CAP))], axis=-1)
    column_range = jnp.arange(columns, dtype=jnp.int32)
    scores = jax.random.randint(key_score, (BRICKS_X, BRICKS_Y, BLK_DEV, columns), 0, 1 << 20) * columns + column_range
    forced_dir = jnp.where(jnp.arange(BRICKS_X, dtype=jnp.int32) < BRICKS_X - 1, 1, 0)[:, None, None, None]
    forced = (block_range[:, None] == 0) & (column_range >= BLK_DEV) & ((column_range - BLK_DEV) // CAP == forced_dir)
    scores = jnp.where(forced, scores + (1 << 26), scores)
    scores = jnp.where(candidate_fine, scores, -1 - column_range)
    _, picked = lax.top_k(scores, NB)
    chosen = jnp.take_along_axis(candidates, picked, axis=-1)
    first_count = jax.random.randint(key_first, (BRICKS_X, BRICKS_Y, BLK_DEV), 1, NB + 1)
    second_count = jax.random.randint(key_second, (BRICKS_X, BRICKS_Y, BLK_DEV), 1, NB + 1)
    counts = jnp.maximum(first_count, second_count)
    counts = jnp.where(block_range == 0, NB, jnp.where(block_range == BLK_DEV - 1, 1, counts))
    listed = jnp.where(jnp.arange(NB, dtype=jnp.int32) < counts[..., None], chosen, own_ids[..., None])
    return (listed.astype(jnp.int32), counts.astype(jnp.int32))


def draw_neighbour_ids(key, part):
    listed, _ = neighbour_tables(key)
    return listed


def draw_neighbour_count(key, part):
    _, counts = neighbour_tables(key)
    return counts


def draw_tokens(key, part):
    row_shape = (BRICKS_X, BRICKS_Y, TOK_DEV, D)
    key_base = jax.random.fold_in(jax.random.fold_in(key, 5), 0)
    key_scale = jax.random.fold_in(jax.random.fold_in(key, 5), 2)
    row_scale = jnp.exp(jax.random.uniform(key_scale, (BRICKS_X, BRICKS_Y, TOK_DEV, 1), jnp.float32, -1.0, 1.0))
    token_rows = jax.random.normal(key_base, row_shape, jnp.float32) * row_scale
    return jnp.clip(token_rows, -6.0, 6.0).astype(jnp.bfloat16)


def draw_w_query_key(key, part):
    key_query, key_key = jax.random.split(jax.random.fold_in(key, 11), 2)
    spread = D ** (-0.5)
    w_query = jax.random.normal(key_query, (D, D), jnp.float32) * spread
    w_key = jax.random.normal(key_key, (D, D), jnp.float32) * spread
    return jnp.concatenate([w_query, w_key], axis=1).astype(jnp.bfloat16)


def shard_levels(key, shape, cuts, least, largest):
    def one(dim, shards_of):
        steps = jax.random.uniform(jax.random.fold_in(jax.random.fold_in(key, 6), dim), (shards_of,), jnp.float32, least / len(cuts), largest / len(cuts))
        return jnp.repeat(jnp.exp(steps), shape[dim] // shards_of).reshape((-1,) + (1,) * (len(shape) - dim - 1))

    gain = one(*cuts[0])
    for cut in cuts[1:]:
        gain = gain * one(*cut)
    return gain


def noise(rng, dims, scale, bound, pieces=(), held_as=jnp.bfloat16):
    gain = shard_levels(rng, dims, pieces, -0.22, 0.18) if pieces else 1.0
    values = jax.random.normal(rng, dims, jnp.float32) * scale * gain
    return jnp.minimum(jnp.maximum(values, -bound), bound).astype(held_as)


def setup_inputs(seed: int = 0) -> dict:
    arg_keys = jax.random.split(jax.random.key(seed), 10)
    tokens = draw_tokens(jax.random.fold_in(arg_keys[9], 71), 0)
    norm_gain = jnp.clip(1.0 + 0.18 * jax.random.normal(arg_keys[1], (D,), jnp.float32), 0.1, 1.9)
    w_query_key = draw_w_query_key(jax.random.fold_in(arg_keys[9], 71), 0)
    w_value = noise(arg_keys[3], (D, D), (D // 16) ** -0.5, 1.0)
    w_out = noise(arg_keys[4], (D, D), D ** -0.5, 0.25)
    cotangent = noise(arg_keys[5], (BRICKS_X, BRICKS_Y, TOK_DEV, D), 1.0, 6.0, ((0, 16), (1, 8)))
    block_order = jax.vmap(lambda own: jax.random.permutation(own, TOK_DEV))(jax.random.split(arg_keys[6], BRICKS_X * BRICKS_Y)).reshape((BRICKS_X, BRICKS_Y, TOK_DEV)).astype(jnp.int32)
    neighbour_ids = draw_neighbour_ids(jax.random.fold_in(arg_keys[9], 71), 0)
    neighbour_count = draw_neighbour_count(jax.random.fold_in(arg_keys[9], 71), 0)
    return dict(tokens=tokens, norm_gain=norm_gain, w_query_key=w_query_key, w_value=w_value, w_out=w_out, cotangent=cotangent, block_order=block_order, neighbour_ids=neighbour_ids, neighbour_count=neighbour_count)


EPSILON = 1e-06

def rms_rows(token_rows, gain_row):
    values = token_rows.astype(jnp.float32)
    inv_rms = lax.rsqrt(lax.optimization_barrier(jnp.mean(values * values, axis=-1, keepdims=True)) + EPSILON)
    return (values, inv_rms, (values * inv_rms * gain_row).astype(jnp.bfloat16))

def attend_block(query_rows, key_value_rows, live_cols, grad_context):
    features = query_rows.shape[-1]
    head_size = features // HEADS
    row_count = query_rows.shape[0]
    factor = 1.0 / math.sqrt(head_size)
    highest = lax.Precision.HIGHEST
    queries = query_rows.reshape(row_count, HEADS, head_size).astype(jnp.float32)
    kv_rows = key_value_rows.reshape(-1, 2 * features)
    key_rows = kv_rows[:, :features].reshape(-1, HEADS, head_size).astype(jnp.float32)
    value_rows = kv_rows[:, features:].reshape(-1, HEADS, head_size).astype(jnp.float32)
    grad_rows = grad_context.reshape(row_count, HEADS, head_size).astype(jnp.float32)
    scores = jnp.einsum('ihd,jhd->hij', queries, key_rows, precision=highest) * factor
    scores = jnp.where(live_cols[None, None, :], scores, -1e+30)
    row_max = lax.optimization_barrier(jnp.max(scores, axis=-1, keepdims=True))
    powers = jnp.exp(scores - row_max)
    attn_probs = powers / lax.optimization_barrier(jnp.sum(powers, axis=-1, keepdims=True))
    probs_low = attn_probs.astype(jnp.bfloat16)
    context = jnp.einsum('hij,jhd->ihd', probs_low.astype(jnp.float32), value_rows, precision=highest).astype(jnp.bfloat16)
    grad_probs = jnp.einsum('ihd,jhd->hij', grad_rows, value_rows, precision=highest)
    centre = lax.optimization_barrier(jnp.sum(attn_probs * grad_probs, axis=-1, keepdims=True))
    grad_scores = (attn_probs * (grad_probs - centre) * factor).astype(jnp.bfloat16)
    grad_query = jnp.einsum('hij,jhd->ihd', grad_scores.astype(jnp.float32), key_rows, precision=highest).astype(jnp.bfloat16)
    grad_keys = jnp.einsum('hij,ihd->jhd', grad_scores.astype(jnp.float32), queries, precision=highest)
    grad_values = jnp.einsum('hij,ihd->jhd', probs_low.astype(jnp.float32), grad_rows, precision=highest)
    slots = key_value_rows.shape[0]
    return (context.reshape(row_count, features), grad_query.reshape(row_count, features), grad_keys.reshape(slots, row_count, features), grad_values.reshape(slots, row_count, features))

def reference(tokens, norm_gain, w_query_key, w_value, w_out, cotangent, block_order, neighbour_ids, neighbour_count):
    bricks = BRICKS_X * BRICKS_Y
    features = D
    row_order = block_order.reshape(bricks, TOK_DEV)
    sorted_rows = jnp.take_along_axis(tokens.reshape(bricks, TOK_DEV, features), row_order[:, :, None], axis=1).reshape(-1, features)
    sorted_grad = jnp.take_along_axis(cotangent.reshape(bricks, TOK_DEV, features), row_order[:, :, None], axis=1).reshape(-1, features)
    values, inv_rms, normed = rms_rows(sorted_rows, norm_gain)
    query_rows = jnp.dot(normed, w_query_key[:, :features], preferred_element_type=jnp.float32).astype(jnp.bfloat16)
    w_pair = jnp.concatenate([w_query_key[:, features:], w_value], axis=1)
    key_value = jnp.dot(normed, w_pair, preferred_element_type=jnp.float32).astype(jnp.bfloat16)
    key_value = key_value.reshape(bricks * BLK_DEV, BLK, 2 * features)
    d_context = jnp.dot(sorted_grad, w_out.T, preferred_element_type=jnp.float32).astype(jnp.bfloat16)
    all_ids = neighbour_ids.reshape(bricks, BLK_DEV, NB)
    all_counts = neighbour_count.reshape(bricks, BLK_DEV)
    query_blocks = query_rows.reshape(bricks, BLK_DEV, BLK, features)
    grad_blocks = d_context.reshape(bricks, BLK_DEV, BLK, features)
    entries = BLK_DEV * (NB + 1)

    def per_block(block_item):
        block_query, block_grad, key_ids, live_slots = block_item
        live_cols = jnp.repeat(live_slots, BLK)
        return attend_block(block_query, key_value[key_ids], live_cols, block_grad)

    def per_brick(grad_total, brick_item):
        brick, brick_query, brick_grad, brick_ids, brick_count = brick_item
        own_ids = brick * BLK_DEV + jnp.arange(BLK_DEV, dtype=jnp.int32)
        key_ids = jnp.concatenate([own_ids[:, None], brick_ids.astype(jnp.int32)], axis=1)
        live_slots = jnp.concatenate([jnp.ones((BLK_DEV, 1), dtype=jnp.bool_), jnp.arange(NB, dtype=jnp.int32)[None, :] < brick_count[:, None]], axis=1)
        context, grad_query, key_terms, value_terms = lax.map(per_block, (brick_query, brick_grad, key_ids, live_slots))
        flat_ids = key_ids.reshape(entries)
        flat_terms = jnp.concatenate([key_terms, value_terms], axis=-1).reshape(entries, BLK * 2 * features)
        same_block = (flat_ids[:, None] == flat_ids[None, :]).astype(jnp.float32)
        summed = jnp.dot(same_block, flat_terms, precision=lax.Precision.HIGHEST)
        earlier = lax.optimization_barrier(jnp.sum(jnp.tril(same_block, -1), axis=1))
        owned = flat_ids // BLK_DEV == brick
        shipped = lax.optimization_barrier(summed.astype(jnp.bfloat16)).astype(jnp.float32)
        partial_sums = jnp.where(owned[:, None], summed, shipped)
        partial_sums = jnp.where((earlier == 0)[:, None], partial_sums, jnp.zeros_like(partial_sums))
        grad_total = grad_total.at[flat_ids].add(partial_sums.reshape(entries, BLK, 2 * features))
        return (grad_total, (context, grad_query))
    start_total = jnp.zeros((bricks * BLK_DEV, BLK, 2 * features), jnp.float32)
    grad_total, (context, grad_query) = lax.scan(per_brick, start_total, (jnp.arange(bricks, dtype=jnp.int32), query_blocks, grad_blocks, all_ids, all_counts))
    grad_kv = grad_total.astype(jnp.bfloat16).reshape(-1, 2 * features)
    context = context.reshape(-1, features)
    grad_query = grad_query.reshape(-1, features)
    out_rows = jnp.dot(context, w_out, preferred_element_type=jnp.float32).astype(jnp.bfloat16)
    grad_w_out = jnp.dot(context.T, sorted_grad, preferred_element_type=jnp.float32)
    grad_proj = jnp.concatenate([grad_query, grad_kv], axis=1)
    w_all = jnp.concatenate([w_query_key, w_value], axis=1)
    grad_normed = jnp.dot(grad_proj, w_all.T, preferred_element_type=jnp.float32)
    grad_all = jnp.dot(normed.T, grad_proj, preferred_element_type=jnp.float32)
    grad_norm_gain = lax.optimization_barrier(jnp.sum(grad_normed * (values * inv_rms), axis=0))
    scaled_grad = grad_normed * norm_gain
    grad_rows = inv_rms * scaled_grad - values * (inv_rms * inv_rms * inv_rms) * lax.optimization_barrier(jnp.mean(values * scaled_grad, axis=-1, keepdims=True))
    inverse = jnp.argsort(row_order, axis=1).astype(jnp.int32)
    branch_out = jnp.take_along_axis(out_rows.reshape(bricks, TOK_DEV, features), inverse[:, :, None], axis=1)
    grad_tokens = jnp.take_along_axis(grad_rows.reshape(bricks, TOK_DEV, features), inverse[:, :, None], axis=1)
    return (branch_out.reshape(BRICKS_X, BRICKS_Y, TOK_DEV, features), grad_tokens.reshape(BRICKS_X, BRICKS_Y, TOK_DEV, features), grad_all[:, :2 * features], grad_all[:, 2 * features:], grad_w_out, grad_norm_gain)
```

```python
import functools

import jax
import jax.numpy as jnp
from jax import lax
from jax.experimental import pallas as pl
from jax.experimental.pallas import tpu as pltpu
from jax.sharding import PartitionSpec as P

BLK = 256
PAIR = 128
EPSILON = 1e-06
BF = jnp.bfloat16
F32 = jnp.float32
MIB = 1 << 20
VM = pl.BlockSpec(memory_space=pltpu.VMEM)
SM = pl.BlockSpec(memory_space=pltpu.SMEM)
NT = (((1,), (1,)), ((), ()))


def mm(a, b):
    return jnp.dot(a, b, preferred_element_type=F32)


def mm_nt(a, b):
    return lax.dot_general(a, b, NT, preferred_element_type=F32)


def rms(rows):
    values = rows.astype(F32)
    inv = lax.rsqrt(jnp.mean(values * values, axis=-1, keepdims=True) + EPSILON)
    return values, inv


def named_mask(ids, cnt, reader, owner, blocks, slots):
    mask = jnp.int32(0)
    for b in range(blocks):
        count = cnt[reader * blocks + b]
        for j in range(slots):
            entry = ids[(reader * blocks + b) * slots + j]
            hit = jnp.logical_and(j < count, lax.div(entry, blocks) == owner)
            mask = mask | jnp.where(hit, jnp.left_shift(1, lax.rem(entry, blocks)), 0)
    return mask


def first_two(mask, blocks):
    def lowest(m):
        at = jnp.int32(blocks - 1)
        for b in range(blocks - 2, -1, -1):
            at = jnp.where((m & (1 << b)) != 0, b, at)
        return at

    first = lowest(mask)
    return first, lowest(mask & ~jnp.left_shift(1, first))


def send_table(ids, cnt, pos, extent_x, extent_y, blocks, slots):
    x, y = pos[0], pos[1]
    me = x * extent_y + y
    readers = (
        jnp.minimum(x + 1, extent_x - 1) * extent_y + y,
        jnp.maximum(x - 1, 0) * extent_y + y,
        x * extent_y + jnp.minimum(y + 1, extent_y - 1),
        x * extent_y + jnp.maximum(y - 1, 0),
    )
    return [first_two(named_mask(ids, cnt, r, me, blocks, slots), blocks) for r in readers]


def pool_table(ids, cnt, pos, extent_y, blocks, slots):
    me = pos[0] * extent_y + pos[1]
    owners = (me - extent_y, me + extent_y, me - 1, me + 1)
    masks = [named_mask(ids, cnt, me, o, blocks, slots) for o in owners]
    table = []
    for b in range(blocks):
        row = []
        for j in range(slots):
            entry = ids[(me * blocks + b) * slots + j]
            owner, off = lax.div(entry, blocks), lax.rem(entry, blocks)
            at = off
            for seg, (o, mask) in enumerate(zip(owners, masks)):
                below = mask & (jnp.left_shift(1, off) - 1)
                at = jnp.where(owner == o, blocks + 2 * seg + jnp.where(below != 0, 1, 0), at)
            live = j < cnt[me * blocks + b]
            row.append((jnp.where(live, at, b), live))
        table.append(row)
    return table


def order_columns(order_ref):
    n = order_ref.shape[1]
    return jnp.broadcast_to(order_ref[...], (128, n)).T


def one_hot_rows(cols, n):
    lane = lax.broadcasted_iota(jnp.int32, cols.shape, 1)
    return jnp.concatenate(
        [(cols == lane + c).astype(F32).astype(BF) for c in range(0, n, 128)], axis=1
    )


def one_hot_back(order_ref, start, rows):
    n = order_ref.shape[1]
    row = lax.broadcasted_iota(jnp.int32, (rows, n), 0) + start
    return (row == order_ref[...]).astype(F32).astype(BF)


def sort_kernel(dims, pos, ids, cnt, order, tok, out, s0, s1, s2, s3, cols):
    extent_x, extent_y, blocks, slots = dims
    n = tok.shape[0]
    cols[...] = order_columns(order)

    def body(b, _):
        rows = pl.ds(pl.multiple_of(b * BLK, BLK), BLK)
        out[rows, :] = mm(one_hot_rows(cols[rows, :], n), tok[...]).astype(BF)
        return 0

    lax.fori_loop(0, n // BLK, body, 0)
    table = send_table(ids, cnt, pos, extent_x, extent_y, blocks, slots)
    for ref, pair in zip((s0, s1, s2, s3), table):
        for k, b in enumerate(pair):
            ref[k * BLK : (k + 1) * BLK, :] = out[pl.ds(pl.multiple_of(b * BLK, BLK), BLK), :]


def project_kernel(groups, np_, order, tok, cot, gain, w_qk, w_v, w_out, *rest):
    sc, n_t = rest[:2]
    outs = rest[2:-1]
    cols = rest[-1]
    d = tok.shape[1]
    n = tok.shape[0]
    cols[...] = order_columns(order)
    per = 8

    def body(b, _):
        rows = pl.ds(pl.multiple_of(b * BLK, BLK), BLK)
        grad = mm(one_hot_rows(cols[rows, :], n), cot[...]).astype(BF)
        sc[b] = grad
        values, inv = rms(tok[rows, :])
        normed = (values * inv * gain[...]).astype(BF)
        n_t[b] = normed.T
        query = (mm(normed, w_qk[:, :d]).astype(BF)) * BF(0.125)
        key = mm(normed, w_qk[:, d:]).astype(BF)
        value = mm(normed, w_v[...]).astype(BF)
        dctx = mm_nt(grad, w_out[...]).astype(BF)
        for at, mat in enumerate((query, key, value, dctx)):
            mat_t = mat.T
            for g in range(groups):
                for p in range(np_):
                    lo = (g * np_ + p) * PAIR
                    outs[g * per + 2 * at][b, p] = mat[:, lo : lo + PAIR]
                    outs[g * per + 2 * at + 1][b, p] = mat_t[lo : lo + PAIR, :]
        return 0

    lax.fori_loop(0, n // BLK, body, 0)


def attend_kernel(dims, np_, pos, ids, cnt, r0, r1, r2, r3, gain, w_k, w_v,
                  qn, qt, kn, kt, vn, vt, gn, gt,
                  ctx_t, dq_t, own, h0, h1, h2, h3, n_t,
                  pkn, pkt, pvn, pvt, acc, s_scr, dp_scr, p_scr, ds_scr, where_ref):
    extent_x, extent_y, blocks, slots = dims
    table = pool_table(ids, cnt, pos, extent_y, blocks, slots)
    for b in range(blocks):
        for j in range(slots):
            where_ref[b * slots + j] = table[b][j][0]
            where_ref[blocks * slots + b * slots + j] = table[b][j][1].astype(jnp.int32)
    for own_ref, pool in ((kn, pkn), (kt, pkt), (vn, pvn), (vt, pvt)):
        pool[:blocks] = own_ref[...]
    for seg, ref in enumerate((r0, r1, r2, r3)):
        for k in range(2):
            at = blocks + 2 * seg + k
            values, inv = rms(ref[k * BLK : (k + 1) * BLK, :])
            normed = (values * inv * gain[...]).astype(BF)
            n_t[2 * seg + k] = normed.T
            for w, nat, tra in ((w_k, pkn, pkt), (w_v, pvn, pvt)):
                made = mm(normed, w[...]).astype(BF)
                made_t = made.T
                for p in range(np_):
                    nat[at, p] = made[:, p * PAIR : (p + 1) * PAIR]
                    tra[at, p] = made_t[p * PAIR : (p + 1) * PAIR, :]
    acc[...] = jnp.zeros_like(acc)
    lane = lax.broadcasted_iota(jnp.int32, (1, PAIR), 1)
    low_lanes = (lane < PAIR // 2).astype(F32).astype(BF)
    high_lanes = (lane >= PAIR // 2).astype(F32).astype(BF)
    half = PAIR // 2

    def diagonal(mat):
        zero = jnp.zeros((half, BLK), BF)
        return jnp.concatenate(
            [jnp.concatenate([mat[:half], zero], axis=1), jnp.concatenate([zero, mat[half:]], axis=1)],
            axis=0,
        )

    def body(step, _):
        b, p = lax.div(step, np_), lax.rem(step, np_)
        q_diag, g_diag = diagonal(qt[b, p]), diagonal(gt[b, p])
        at = [b] + [where_ref[b * slots + j] for j in range(slots)]
        live = [None] + [where_ref[blocks * slots + b * slots + j] for j in range(slots)]
        top = None
        for j in range(slots + 1):
            s = mm(pkn[at[j], p], q_diag)
            if j:
                s = jnp.where(live[j] != 0, s, -1e30)
            s_scr[j] = s
            m = jnp.max(s, axis=0, keepdims=True)
            top = m if top is None else jnp.maximum(top, m)
        total = jnp.zeros((1, 2 * BLK), F32)
        centre = jnp.zeros((1, 2 * BLK), F32)
        for j in range(slots + 1):
            e = jnp.exp(s_scr[j] - top)
            s_scr[j] = e
            total += jnp.sum(e, axis=0, keepdims=True)
            dp = mm(pvn[at[j], p], g_diag)
            dp_scr[j] = dp
            centre += jnp.sum(e * dp, axis=0, keepdims=True)
        scale = 1.0 / total
        centre = centre * scale
        for j in range(slots + 1):
            prob = s_scr[j] * scale
            p_scr[j] = prob.astype(BF)
            ds_scr[j] = (prob * (dp_scr[j] - centre)).astype(BF)
        q_rows = qn[b, p]
        g_rows = gn[b, p]
        q_mask = jnp.concatenate([q_rows * low_lanes, q_rows * high_lanes], axis=0)
        g_mask = jnp.concatenate([g_rows * low_lanes, g_rows * high_lanes], axis=0)
        for h in range(2):
            feats, lanes = slice(h * half, (h + 1) * half), slice(h * BLK, (h + 1) * BLK)
            ctx = dq = None
            for j in range(slots + 1):
                c = mm(pvt[at[j], p, feats, :], p_scr[j, :, lanes])
                k = mm(pkt[at[j], p, feats, :], ds_scr[j, :, lanes])
                ctx = c if ctx is None else ctx + c
                dq = k if dq is None else dq + k
            rows = pl.ds(pl.multiple_of(p * PAIR + h * half, half), half)
            ctx_t[b, rows, :] = ctx.astype(BF)
            dq_t[b, rows, :] = (dq * 0.125).astype(BF)
        for j in range(slots + 1):
            acc[at[j], 0, p] += mm(ds_scr[j], q_mask)
            acc[at[j], 1, p] += mm(p_scr[j], g_mask)
        return 0

    lax.fori_loop(0, blocks * np_, body, 0)
    own[...] = acc[:blocks]
    for seg, ref in enumerate((h0, h1, h2, h3)):
        ref[...] = acc[blocks + 2 * seg : blocks + 2 * seg + 2].astype(BF)


def weights_kernel(np_, gain, w_qk, w_v, sc, n_t, far_t, ctx_t, dq_t, own, h0, h1, h2, h3,
                   out, gain_out, rows_scr, nt_scr):
    blocks = n_t.shape[0]
    d = w_v.shape[0]
    for b in range(blocks):
        nt_scr[:, b * BLK : (b + 1) * BLK] = n_t[b]
    for b in range(far_t.shape[0]):
        at = blocks + b
        nt_scr[:, at * BLK : (at + 1) * BLK] = far_t[b]
    for part in range(2):
        for p in range(np_):
            lanes = slice(p * PAIR, (p + 1) * PAIR)
            for b in range(blocks):
                rows_scr[part, b * BLK : (b + 1) * BLK, lanes] = own[b, part, p].astype(BF)
            for seg, ref in enumerate((h0, h1, h2, h3)):
                for k in range(2):
                    at = blocks + 2 * seg + k
                    rows_scr[part, at * BLK : (at + 1) * BLK, lanes] = ref[k, part, p]
    g_q = None
    g_o = None
    for b in range(blocks):
        a = mm_nt(n_t[b], dq_t[b])
        c = mm(ctx_t[b], sc[b])
        g_q = a if g_q is None else g_q + a
        g_o = c if g_o is None else g_o + c
    out[0] = g_q.astype(BF)
    out[3] = g_o.astype(BF)
    g_k = mm(nt_scr[...], rows_scr[0])
    out[1] = g_k.astype(BF)
    g_v = mm(nt_scr[...], rows_scr[1])
    out[2] = g_v.astype(BF)
    total = (
        jnp.sum(g_q * w_qk[:, :d].astype(F32), axis=1, keepdims=True)
        + jnp.sum(g_k * w_qk[:, d:].astype(F32), axis=1, keepdims=True)
        + jnp.sum(g_v * w_v[...].astype(F32), axis=1, keepdims=True)
    )
    gain_out[...] = jnp.broadcast_to(total, (d, 128)).T[:8] / gain[...]


def output_kernel(order, w_qk, w_out, ctx_t, dq_t, out, part):
    blocks, d = ctx_t.shape[:2]

    def body(a, _):
        rows = pl.ds(pl.multiple_of(a * BLK, BLK), BLK)
        back = one_hot_back(order, a * BLK, BLK)
        ctx = dq = None
        for b in range(blocks):
            pick = back[:, b * BLK : (b + 1) * BLK]
            c, k = mm_nt(pick, ctx_t[b]), mm_nt(pick, dq_t[b])
            ctx = c if ctx is None else ctx + c
            dq = k if dq is None else dq + k
        out[rows, :] = mm(ctx.astype(BF), w_out[...]).astype(BF)
        part[rows, :] = mm_nt(dq.astype(BF), w_qk[:, :d])
        return 0

    lax.fori_loop(0, out.shape[0] // BLK, body, 0)


def rows_kernel(dims, np_, pos, ids, cnt, order, tok, gain, w_qk, w_v, part, own, b0, b1, b2, b3,
                out, acc, rows_scr):
    extent_x, extent_y, blocks, slots = dims
    d = w_v.shape[0]
    acc[...] = own[...]
    table = send_table(ids, cnt, pos, extent_x, extent_y, blocks, slots)
    for ref, pair in zip((b0, b1, b2, b3), table):
        for k, b in enumerate(pair):
            acc[b] += ref[k].astype(F32)
    for half in range(2):
        for p in range(np_):
            lo = half * d + p * PAIR
            for b in range(blocks):
                rows_scr[b * BLK : (b + 1) * BLK, lo : lo + PAIR] = acc[b, half, p].astype(BF)

    def body(a, _):
        rows = pl.ds(pl.multiple_of(a * BLK, BLK), BLK)
        back = one_hot_back(order, a * BLK, BLK)
        mine = mm(back, rows_scr[...]).astype(BF)
        grad = part[rows, :] + mm_nt(mine[:, :d], w_qk[:, d:]) + mm_nt(mine[:, d:], w_v[...])
        values, inv = rms(tok[rows, :])
        u = grad * gain[...]
        mean = jnp.mean(values * u, axis=-1, keepdims=True)
        out[rows, :] = inv * u - values * (inv * inv * inv * mean)
        return 0

    lax.fori_loop(0, out.shape[0] // BLK, body, 0)


def step_to(block, axis, distance):
    n = lax.axis_size(axis)
    route = [(i, i + distance) for i in range(n) if 0 <= i + distance < n]
    return lax.ppermute(block, axis, route)


def stage_of(axis, stride, count):
    n = lax.axis_size(axis)
    me = lax.rem(lax.div(lax.axis_index(axis), stride), count)

    def route(s):
        pairs = []
        for i in range(n):
            k = (i // stride) % count
            pairs.append((i, i + (((k + s) % count) - k) * stride))
        return pairs

    return me, route


def scatter_sum(rows, gain, stage, axis, kind):
    me, route = stage
    count = stage_count(stage)
    size = rows.shape[0] // count
    pad = 16
    sent = []
    tail = jnp.broadcast_to(gain, (pad, gain.shape[1])).astype(kind)
    for s in range(1, count):
        to = lax.rem(me + s, count)
        part = lax.dynamic_slice_in_dim(rows, to * size, size).astype(kind)
        sent.append(lax.ppermute(jnp.concatenate([part, tail], axis=0), axis, route(s)))
    total = lax.dynamic_slice_in_dim(rows, me * size, size).astype(F32)
    for r in sent:
        total = total + r[:size].astype(F32)
        gain = gain + r[size : size + 1].astype(F32)
    return total, gain


def gather_all(rows, stage, axis):
    me, route = stage
    count = stage_count(stage)
    size = rows.shape[0]
    out = jnp.zeros((count * size, rows.shape[1]), rows.dtype)
    out = lax.dynamic_update_slice_in_dim(out, rows, me * size, 0)
    for s in range(1, count):
        got = lax.ppermute(rows, axis, route(s))
        out = lax.dynamic_update_slice_in_dim(out, got, lax.rem(me - s + count, count) * size, 0)
    return out


def stage_count(stage):
    return stage[1].count


def make_stage(axis, stride, count):
    me, route = stage_of(axis, stride, count)
    route.count = count
    return me, route


def call(kernel, name, outs, ins, specs, scratch, limit, flops, moved, exps=0):
    return pl.pallas_call(
        kernel,
        out_shape=outs,
        in_specs=specs,
        out_specs=jax.tree.map(lambda _: VM, outs),
        scratch_shapes=scratch,
        compiler_params=pltpu.CompilerParams(vmem_limit_bytes=limit * MIB),
        cost_estimate=pl.CostEstimate(flops=flops, bytes_accessed=moved, transcendentals=exps),
        name=name,
    )(*ins)


def shards(tokens, norm_gain, w_query_key, w_value, w_out, cotangent, block_order,
           neighbour_ids, neighbour_count):
    n, d = tokens.shape[2:]
    extent_x, extent_y, blocks, slots = neighbour_ids.shape
    dims = (extent_x, extent_y, blocks, slots)
    groups = 1
    np_ = d // PAIR // groups
    tok, cot = tokens[0, 0], cotangent[0, 0]
    order = block_order[0]
    gain = norm_gain[None, :]
    ids = neighbour_ids.reshape(-1)
    cnt = neighbour_count.reshape(-1)
    pos = jnp.stack([lax.axis_index("bx"), lax.axis_index("by")]).astype(jnp.int32)
    shape = jax.ShapeDtypeStruct

    sends = [shape((2 * BLK, d), BF)] * 4
    sorted_rows, *sent = call(
        functools.partial(sort_kernel, dims), "sort_rows",
        [shape((n, d), BF)] + sends, (pos, ids, cnt, order, tok), [SM, SM, SM, VM, VM],
        [pltpu.VMEM((n, 128), jnp.int32)], 32, 2 * n * n * d, 4 << 20,
    )
    arrived = [
        step_to(sent[0], "bx", 1), step_to(sent[1], "bx", -1),
        step_to(sent[2], "by", 1), step_to(sent[3], "by", -1),
    ]
    nat, tra = shape((blocks, np_, BLK, PAIR), BF), shape((blocks, np_, PAIR, BLK), BF)
    sc, n_t, *made = call(
        functools.partial(project_kernel, groups, np_), "project",
        [shape((blocks, BLK, d), BF), shape((blocks, d, BLK), BF)] + [nat, tra] * (4 * groups),
        (order, sorted_rows, cot, gain, w_query_key, w_value, w_out), [VM] * 7,
        [pltpu.VMEM((n, 128), jnp.int32)], 40, 2 * n * n * d + 8 * n * d * d, 14 << 20,
    )
    pool = blocks + 8
    back = [shape((2, 2, np_, BLK, PAIR), BF)] * 4
    tile = (slots + 1, BLK, 2 * BLK)
    ctx_t, dq_t, own, h0, h1, h2, h3, far_t = call(
        functools.partial(attend_kernel, dims, np_), "attend",
        [shape((blocks, d, BLK), BF)] * 2 + [shape((blocks, 2, np_, BLK, PAIR), F32)] + back
        + [shape((8, d, BLK), BF)],
        (pos, ids, cnt, *arrived, gain, w_query_key[:, d:], w_value, *made),
        [SM] * 3 + [VM] * 15,
        [pltpu.VMEM((pool, np_, BLK, PAIR), BF), pltpu.VMEM((pool, np_, PAIR, BLK), BF)] * 2
        + [pltpu.VMEM((pool, 2, np_, BLK, PAIR), F32), pltpu.VMEM(tile, F32), pltpu.VMEM(tile, F32),
           pltpu.VMEM(tile, BF), pltpu.VMEM(tile, BF), pltpu.SMEM((2 * blocks * slots,), jnp.int32)],
        60, 12 * blocks * 5 * BLK * BLK * d, 24 << 20, blocks * 5 * BLK * BLK * 8,
    )
    returned = [
        step_to(h0, "bx", -1), step_to(h1, "bx", 1), step_to(h2, "by", -1), step_to(h3, "by", 1),
    ]
    terms, gain_term = call(
        functools.partial(weights_kernel, np_), "weight_terms",
        [shape((4, d, d), BF), shape((8, d), F32)],
        (gain, w_query_key, w_value, sc, n_t, far_t, ctx_t, dq_t, own, h0, h1, h2, h3), [VM] * 13,
        [pltpu.VMEM((2, pool * BLK, d), BF), pltpu.VMEM((d, pool * BLK), BF)],
        56, 4 * n * d * d + 4 * pool * BLK * d * d, 20 << 20,
    )
    branch_out, part = call(
        output_kernel, "branch_rows", [shape((n, d), BF), shape((n, d), F32)],
        (order, w_query_key, w_out, ctx_t, dq_t), [VM] * 5, [], 40,
        4 * n * n * d + 4 * n * d * d, 7 << 20,
    )

    stages = [("by", 1, 2), ("by", 2, 4), ("bx", 1, 4), ("bx", 4, 4)]
    made_stages = [make_stage(*s) for s in stages]
    rows, gain_sum = terms.reshape(4 * d, d), gain_term[:1]
    for (axis, _, _), stage, kind in zip(stages, made_stages, (BF, BF, F32, F32)):
        rows, gain_sum = scatter_sum(rows, gain_sum, stage, axis, kind)
    rows = rows.astype(BF)
    for (axis, _, _), stage in reversed(list(zip(stages, made_stages))):
        rows = gather_all(rows, stage, axis)
    grads = rows.reshape(4, d, d).astype(F32)

    b_x1, b_xm, b_y1, b_ym = returned
    grad_rows = call(
        functools.partial(rows_kernel, dims, np_), "token_rows", shape((n, d), F32),
        (pos, ids, cnt, order, tok, gain, w_query_key, w_value, part, own, b_x1, b_xm, b_y1, b_ym),
        [SM] * 3 + [VM] * 11,
        [pltpu.VMEM((blocks, 2, np_, BLK, PAIR), F32), pltpu.VMEM((n, 2 * d), BF)],
        56, 4 * n * n * d + 4 * n * d * d, 16 << 20,
    )
    return (
        branch_out[None, None],
        grad_rows[None, None],
        jnp.concatenate([grads[0], grads[1]], axis=1),
        grads[2],
        grads[3],
        gain_sum[0],
    )


def solution(mesh):
    local = P("bx", "by", None, None)
    placed = (local, P(), P(), P(), P(), local, P("bx", "by", None), P(), P())
    return jax.shard_map(
        shards,
        mesh=mesh,
        in_specs=placed,
        out_specs=(local, local, P(), P(), P(), P()),
        check_vma=False,
    )
```

```python
import functools

import jax
import jax.numpy as jnp
from jax import lax
from jax.experimental import pallas as pl
from jax.experimental.pallas import tpu as pltpu
from jax.sharding import PartitionSpec as P

BLK = 256
PAIR = 128
EPSILON = 1e-06
BF = jnp.bfloat16
F32 = jnp.float32
MIB = 1 << 20
LIMIT = 58
VM = pl.BlockSpec(memory_space=pltpu.VMEM)
SM = pl.BlockSpec(memory_space=pltpu.SMEM)
AN = pl.BlockSpec(memory_space=pl.ANY)
NT = (((1,), (1,)), ((), ()))


def mm(a, b):
    return jnp.dot(a, b, preferred_element_type=F32)


def mm_nt(a, b):
    return lax.dot_general(a, b, NT, preferred_element_type=F32)


def rms(rows):
    values = rows.astype(F32)
    inv = lax.rsqrt(jnp.mean(values * values, axis=-1, keepdims=True) + EPSILON)
    return values, inv


def named_mask(ids, cnt, reader, owner, blocks, slots):
    mask = jnp.int32(0)
    for b in range(blocks):
        count = cnt[reader * blocks + b]
        for j in range(slots):
            entry = ids[(reader * blocks + b) * slots + j]
            hit = jnp.logical_and(j < count, lax.div(entry, blocks) == owner)
            mask = mask | jnp.where(hit, jnp.left_shift(1, lax.rem(entry, blocks)), 0)
    return mask


def first_two(mask, blocks):
    def lowest(m):
        at = jnp.int32(blocks - 1)
        for b in range(blocks - 2, -1, -1):
            at = jnp.where((m & (1 << b)) != 0, b, at)
        return at

    first = lowest(mask)
    return first, lowest(mask & ~jnp.left_shift(1, first))


def send_table(ids, cnt, pos, extent_x, extent_y, blocks, slots):
    x, y = pos[0], pos[1]
    me = x * extent_y + y
    readers = (
        jnp.minimum(x + 1, extent_x - 1) * extent_y + y,
        jnp.maximum(x - 1, 0) * extent_y + y,
        x * extent_y + jnp.minimum(y + 1, extent_y - 1),
        x * extent_y + jnp.maximum(y - 1, 0),
    )
    return [first_two(named_mask(ids, cnt, r, me, blocks, slots), blocks) for r in readers]


def pool_table(ids, cnt, pos, extent_y, blocks, slots):
    me = pos[0] * extent_y + pos[1]
    owners = (me - extent_y, me + extent_y, me - 1, me + 1)
    masks = [named_mask(ids, cnt, me, o, blocks, slots) for o in owners]
    table = []
    for b in range(blocks):
        row = []
        for j in range(slots):
            entry = ids[(me * blocks + b) * slots + j]
            owner, off = lax.div(entry, blocks), lax.rem(entry, blocks)
            at = off
            for seg, (o, mask) in enumerate(zip(owners, masks)):
                below = mask & (jnp.left_shift(1, off) - 1)
                at = jnp.where(owner == o, blocks + 2 * seg + jnp.where(below != 0, 1, 0), at)
            live = j < cnt[me * blocks + b]
            row.append((jnp.where(live, at, b), live))
        table.append(row)
    return table


def order_columns(order_ref):
    n = order_ref.shape[1]
    return jnp.broadcast_to(order_ref[...], (128, n)).T


def one_hot_rows(cols, n):
    lane = lax.broadcasted_iota(jnp.int32, cols.shape, 1)
    return jnp.concatenate(
        [(cols == lane + c).astype(F32).astype(BF) for c in range(0, n, 128)], axis=1
    )


def one_hot_back(order_ref, start, rows):
    n = order_ref.shape[1]
    row = lax.broadcasted_iota(jnp.int32, (rows, n), 0) + start
    return (row == order_ref[...]).astype(F32).astype(BF)


def sort_kernel(dims, pos, ids, cnt, order, tok, out, s0, s1, s2, s3, cols):
    extent_x, extent_y, blocks, slots = dims
    n = tok.shape[0]
    cols[...] = order_columns(order)

    def body(b, _):
        rows = pl.ds(pl.multiple_of(b * BLK, BLK), BLK)
        out[rows, :] = mm(one_hot_rows(cols[rows, :], n), tok[...]).astype(BF)
        return 0

    lax.fori_loop(0, n // BLK, body, 0)
    table = send_table(ids, cnt, pos, extent_x, extent_y, blocks, slots)
    for ref, pair in zip((s0, s1, s2, s3), table):
        for k, b in enumerate(pair):
            ref[k * BLK : (k + 1) * BLK, :] = out[pl.ds(pl.multiple_of(b * BLK, BLK), BLK), :]


def project_kernel(np_, order, tok, cot, gain, w_qk, w_v, w_out, sc, n_t, *rest):
    *outs, cols = rest
    n, d = cot.shape
    b = pl.program_id(0)

    @pl.when(b == 0)
    def _():
        cols[...] = order_columns(order)

    rows = pl.ds(pl.multiple_of(b * BLK, BLK), BLK)
    grad = mm(one_hot_rows(cols[rows, :], n), cot[...]).astype(BF)
    sc[0] = grad
    values, inv = rms(tok[...])
    normed = (values * inv * gain[...]).astype(BF)
    n_t[0] = normed.T
    query = (mm(normed, w_qk[:, :d]).astype(BF)) * BF(0.125)
    key = mm(normed, w_qk[:, d:]).astype(BF)
    value = mm(normed, w_v[...]).astype(BF)
    dctx = mm_nt(grad, w_out[...]).astype(BF)
    for at, mat in enumerate((query, key, value, dctx)):
        mat_t = mat.T
        for p in range(np_):
            outs[2 * at][0, p] = mat[:, p * PAIR : (p + 1) * PAIR]
            outs[2 * at + 1][0, p] = mat_t[p * PAIR : (p + 1) * PAIR, :]


def attend_kernel(dims, np_, pos, ids, cnt, gain, r0, r1, r2, r3, w_qk_in, w_v_in,
                  qn_in, qt_in, kn_in, kt_in, vn_in, vt_in, gn_in, gt_in, sc_in, nt_in,
                  ctx_out, dq_out, own, h0, h1, h2, h3, keep, send, gain_out,
                  far, w_qk, w_v, qn, qt, gn, gt, pkn, pkt, pvn, pvt, sc, n_t, ctx_t, dq_t, acc,
                  s_scr, dp_scr, p_scr, ds_scr, terms, where_ref, sem_in, sem_out):
    extent_x, extent_y, blocks, slots = dims
    d = w_v.shape[0]
    mine = pl.ds(0, blocks)
    first, later = [], []

    def fetch(src, dst, into):
        copy = pltpu.make_async_copy(src, dst, sem_in.at[len(first) + len(later)])
        copy.start()
        into.append(copy)

    fetch(w_qk_in, w_qk, first)
    fetch(w_v_in, w_v, first)
    for seg, ref in enumerate((r0, r1, r2, r3)):
        fetch(ref, far.at[seg], first)
    for src, dst in ((kn_in, pkn.at[mine]), (kt_in, pkt.at[mine]), (vn_in, pvn.at[mine]),
                     (vt_in, pvt.at[mine]), (qt_in, qt), (gt_in, gt), (qn_in, qn), (gn_in, gn),
                     (nt_in, n_t.at[mine]), (sc_in, sc)):
        fetch(src, dst, later)
    table = pool_table(ids, cnt, pos, extent_y, blocks, slots)
    for b in range(blocks):
        for j in range(slots):
            where_ref[b * slots + j] = table[b][j][0]
    acc[...] = jnp.zeros_like(acc)
    for copy in first:
        copy.wait()

    def remote(i, _):
        rows = pl.ds(pl.multiple_of(lax.rem(i, 2) * BLK, BLK), BLK)
        values, inv = rms(far[lax.div(i, 2), rows, :])
        normed = (values * inv * gain[...]).astype(BF)
        n_t[blocks + i] = normed.T
        made = mm(normed, w_qk[:, d:]).astype(BF)
        made_v = mm(normed, w_v[...]).astype(BF)
        for mat, nat, tra in ((made, pkn, pkt), (made_v, pvn, pvt)):
            mat_t = mat.T
            for p in range(np_):
                nat[blocks + i, p] = mat[:, p * PAIR : (p + 1) * PAIR]
                tra[blocks + i, p] = mat_t[p * PAIR : (p + 1) * PAIR, :]
        return 0

    lax.fori_loop(0, 8, remote, 0)
    for copy in later:
        copy.wait()
    lane = lax.broadcasted_iota(jnp.int32, (1, PAIR), 1)
    low_lanes = (lane < PAIR // 2).astype(F32).astype(BF)
    high_lanes = (lane >= PAIR // 2).astype(F32).astype(BF)
    half = PAIR // 2

    def diagonal(mat):
        zero = jnp.zeros((half, BLK), BF)
        return jnp.concatenate(
            [jnp.concatenate([mat[:half], zero], axis=1), jnp.concatenate([zero, mat[half:]], axis=1)],
            axis=0,
        )

    def pair(b, p, at):
        q_diag, g_diag = diagonal(qt[b, p]), diagonal(gt[b, p])
        top = None
        for j, k in enumerate(at):
            s = mm(pkn[k, p], q_diag)
            s_scr[j] = s
            m = jnp.max(s, axis=0, keepdims=True)
            top = m if top is None else jnp.maximum(top, m)
        total = jnp.zeros((1, 2 * BLK), F32)
        centre = jnp.zeros((1, 2 * BLK), F32)
        for j, k in enumerate(at):
            e = jnp.exp(s_scr[j] - top)
            s_scr[j] = e
            total += jnp.sum(e, axis=0, keepdims=True)
            dp = mm(pvn[k, p], g_diag)
            dp_scr[j] = dp
            centre += jnp.sum(e * dp, axis=0, keepdims=True)
        scale = 1.0 / total
        centre = centre * scale
        for j in range(len(at)):
            prob = s_scr[j] * scale
            p_scr[j] = prob.astype(BF)
            ds_scr[j] = (prob * (dp_scr[j] - centre)).astype(BF)
        q_rows = qn[b, p]
        g_rows = gn[b, p]
        q_mask = jnp.concatenate([q_rows * low_lanes, q_rows * high_lanes], axis=0)
        g_mask = jnp.concatenate([g_rows * low_lanes, g_rows * high_lanes], axis=0)
        for h in range(2):
            feats, lanes = slice(h * half, (h + 1) * half), slice(h * BLK, (h + 1) * BLK)
            ctx = dq = None
            for j, k in enumerate(at):
                c = mm(pvt[k, p, feats, :], p_scr[j, :, lanes])
                t = mm(pkt[k, p, feats, :], ds_scr[j, :, lanes])
                ctx = c if ctx is None else ctx + c
                dq = t if dq is None else dq + t
            rows = pl.ds(pl.multiple_of(p * PAIR + h * half, half), half)
            ctx_t[b, rows, :] = ctx.astype(BF)
            dq_t[b, rows, :] = (dq * 0.125).astype(BF)
        for j, k in enumerate(at):
            acc[k, 0, p] += mm(ds_scr[j], q_mask)
            acc[k, 1, p] += mm(p_scr[j], g_mask)

    me = pos[0] * extent_y + pos[1]

    def block(b, _):
        count = cnt[me * blocks + b]
        for live in range(1, slots + 1):

            @pl.when(count == live)
            def _():
                at = [b] + [where_ref[b * slots + j] for j in range(live)]
                lax.fori_loop(0, np_, lambda p, c: (pair(b, p, at), c)[1], 0)

        return 0

    lax.fori_loop(0, blocks, block, 0)
    out = []

    def ship(src, dst):
        copy = pltpu.make_async_copy(src, dst, sem_out.at[len(out)])
        copy.start()
        out.append(copy)

    ship(ctx_t, ctx_out)
    ship(dq_t, dq_out)
    ship(acc.at[mine], own)

    def lower(b, _):
        for p in range(np_):
            pkn[b, p] = acc[b, 0, p].astype(BF)
            pvn[b, p] = acc[b, 1, p].astype(BF)
        return 0

    lax.fori_loop(0, blocks + 8, lower, 0)
    for seg, ref in enumerate((h0, h1, h2, h3)):
        part = pl.ds(blocks + 2 * seg, 2)
        ship(pkn.at[part], ref.at[0])
        ship(pvn.at[part], ref.at[1])
    core = lax.rem(pos[1], 2)
    total = jnp.zeros((d, 1), F32)

    def place(i, value):
        terms[lax.rem(i + core, 2), (i // 2) * BLK : (i // 2 + 1) * BLK, :] = value.astype(BF)

    g_q = g_o = None
    for b in range(blocks):
        a, c = mm_nt(n_t[b], dq_t[b]), mm(ctx_t[b], sc[b])
        g_q = a if g_q is None else g_q + a
        g_o = c if g_o is None else g_o + c
    for i, g in ((0, g_q), (6, g_o)):
        place(i, g[:BLK])
        place(i + 1, g[BLK:])
    total += jnp.sum(g_q * w_qk[:, :d].astype(F32), axis=1, keepdims=True)
    for i, pool, w, lo in ((2, pkn, w_qk, d), (4, pvn, w_v, 0)):
        made = []
        for p in range(0, np_, 2):
            g = None
            for b in range(blocks + 8):
                t = mm(n_t[b], jnp.concatenate([pool[b, p], pool[b, p + 1]], axis=1))
                g = t if g is None else g + t
            at = lo + p * PAIR
            total += jnp.sum(g * w[:, at : at + 2 * PAIR].astype(F32), axis=1, keepdims=True)
            made.append(g)
        g = jnp.concatenate(made, axis=1)
        place(i, g[:BLK])
        place(i + 1, g[BLK:])
    gain_term = jnp.broadcast_to(total, (d, 128)).T[:8] / gain[...]
    gain_out[...] = gain_term
    terms[:, blocks * BLK :, :] = jnp.broadcast_to(gain_term[:1].astype(BF)[None], (2, 16, d))
    ship(terms.at[0, pl.ds(0, blocks * BLK)], keep)
    ship(terms.at[1], send)
    for copy in out:
        copy.wait()


def core_kernel(pos, keep, got, gain, own, s1, s2, s3, gain_out):
    size, d = own.shape
    rows = 4 * size
    total = gain[:1] + got[rows : rows + 1, :].astype(F32)
    gain_out[...] = jnp.broadcast_to(total, gain_out.shape)
    y = lax.div(pos[1], 2)
    for s, ref in enumerate((own, s1, s2, s3)):
        at = pl.ds(pl.multiple_of(lax.rem(y + s, 4) * size, size), size)
        value = keep[at, :].astype(F32) + got[at, :].astype(F32)
        if s:
            ref[:size, :] = value.astype(BF)
            ref[size:, :] = jnp.broadcast_to(total, (ref.shape[0] - size, d)).astype(BF)
        else:
            ref[...] = value


def output_kernel(order, w_qk, w_out, ctx_t, dq_t, out, part):
    blocks, d = ctx_t.shape[0], w_out.shape[0]

    def body(a, _):
        rows = pl.ds(pl.multiple_of(a * BLK, BLK), BLK)
        back = one_hot_back(order, a * BLK, BLK)
        made = []
        for ref in (ctx_t, dq_t):
            total = None
            for b in range(blocks):
                t = mm_nt(back[:, b * BLK : (b + 1) * BLK], ref[b])
                total = t if total is None else total + t
            made.append(total.astype(BF))
        out[rows, :] = mm(made[0], w_out[...]).astype(BF)
        part[rows, :] = mm_nt(made[1], w_qk[:, :d])
        return 0

    lax.fori_loop(0, out.shape[0] // BLK, body, 0)


def rows_kernel(dims, np_, pos, ids, cnt, order, tok, gain, w_qk, w_v, part, own, b0, b1, b2, b3,
                out, acc, rows_scr):
    extent_x, extent_y, blocks, slots = dims
    d = w_v.shape[0]
    acc[...] = own[...]
    table = send_table(ids, cnt, pos, extent_x, extent_y, blocks, slots)
    for ref, pair in zip((b0, b1, b2, b3), table):
        for k, b in enumerate(pair):
            acc[b, 0] += ref[0, k].astype(F32)
            acc[b, 1] += ref[1, k].astype(F32)
    for half in range(2):
        for p in range(np_):
            lo = half * d + p * PAIR
            for b in range(blocks):
                rows_scr[b * BLK : (b + 1) * BLK, lo : lo + PAIR] = acc[b, half, p].astype(BF)

    def body(a, _):
        rows = pl.ds(pl.multiple_of(a * BLK, BLK), BLK)
        back = one_hot_back(order, a * BLK, BLK)
        mine = mm(back, rows_scr[...]).astype(BF)
        grad = part[rows, :] + mm_nt(mine[:, :d], w_qk[:, d:]) + mm_nt(mine[:, d:], w_v[...])
        values, inv = rms(tok[rows, :])
        u = grad * gain[...]
        mean = jnp.mean(values * u, axis=-1, keepdims=True)
        out[rows, :] = inv * u - values * (inv * inv * inv * mean)
        return 0

    lax.fori_loop(0, out.shape[0] // BLK, body, 0)


def place_kernel(rows, qk, v, o):
    d = v.shape[0]
    qk[:, :d] = rows[:d, :].astype(F32)
    qk[:, d:] = rows[d : 2 * d, :].astype(F32)
    v[...] = rows[2 * d : 3 * d, :].astype(F32)
    o[...] = rows[3 * d :, :].astype(F32)


def step_to(block, axis, distance):
    n = lax.axis_size(axis)
    route = [(i, i + distance) for i in range(n) if 0 <= i + distance < n]
    return lax.ppermute(block, axis, route)


def across_x(rows, gain):
    count = lax.axis_size("bx")
    size = rows.shape[0] // count
    extra = jnp.zeros((size, 128), F32).at[: gain.shape[1] // 128].set(gain.reshape(-1, 128))
    extra = jnp.broadcast_to(extra[None], (count, size, 128))
    parts = jnp.concatenate([rows.reshape(count, size, -1), extra], axis=2).astype(BF)
    got = lax.all_to_all(parts, "bx", 0, 0, tiled=True)
    total = jnp.sum(got.astype(F32), axis=0)
    gain = total[: gain.shape[1] // 128, rows.shape[1] :].reshape(1, -1)
    mine = total[:, : rows.shape[1]].astype(BF)
    back = lax.all_to_all(jnp.broadcast_to(mine[None], (count,) + mine.shape), "bx", 0, 0, tiled=True)
    return back.reshape(rows.shape), gain


def call(kernel, name, outs, ins, specs, scratch, limit, flops, moved, exps=0, out_specs=None, grid=()):
    return pl.pallas_call(
        kernel,
        out_shape=outs,
        grid=grid,
        in_specs=specs,
        out_specs=jax.tree.map(lambda _: VM, outs) if out_specs is None else out_specs,
        scratch_shapes=scratch,
        compiler_params=pltpu.CompilerParams(vmem_limit_bytes=limit * MIB),
        cost_estimate=pl.CostEstimate(flops=flops, bytes_accessed=moved, transcendentals=exps),
        name=name,
    )(*ins)


def shards(tokens, norm_gain, w_query_key, w_value, w_out, cotangent, block_order,
           neighbour_ids, neighbour_count):
    n, d = tokens.shape[2:]
    extent_x, extent_y, blocks, slots = neighbour_ids.shape
    dims = (extent_x, extent_y, blocks, slots)
    np_ = d // PAIR
    tok, cot = tokens[0, 0], cotangent[0, 0]
    order = block_order[0]
    gain = norm_gain[None, :]
    ids = neighbour_ids.reshape(-1)
    cnt = neighbour_count.reshape(-1)
    pos = jnp.stack([lax.axis_index("bx"), lax.axis_index("by")]).astype(jnp.int32)
    shape = jax.ShapeDtypeStruct

    sends = [shape((2 * BLK, d), BF)] * 4
    sorted_rows, *sent = call(
        functools.partial(sort_kernel, dims), "sort_rows",
        [shape((n, d), BF)] + sends, (pos, ids, cnt, order, tok), [SM, SM, SM, VM, VM],
        [pltpu.VMEM((n, 128), jnp.int32)], 32, 2 * n * n * d, 4 << 20,
    )
    arrived = [
        step_to(sent[0], "bx", 1), step_to(sent[1], "bx", -1),
        step_to(sent[2], "by", 1), step_to(sent[3], "by", -1),
    ]
    nat, tra = (blocks, np_, BLK, PAIR), (blocks, np_, PAIR, BLK)

    def a_block(dims_):
        return pl.BlockSpec((1,) + dims_[1:], lambda b: (b,) + (0,) * (len(dims_) - 1))

    whole = pl.BlockSpec(memory_space=pltpu.VMEM)
    out_dims = [(blocks, BLK, d), (blocks, d, BLK)] + [nat, tra] * 4
    sc, n_t, *made = call(
        functools.partial(project_kernel, np_), "project", [shape(k, BF) for k in out_dims],
        (order, sorted_rows, cot, gain, w_query_key, w_value, w_out),
        [whole, pl.BlockSpec((BLK, d), lambda b: (b, 0))] + [whole] * 5,
        [pltpu.VMEM((n, 128), jnp.int32)], LIMIT, 2 * n * n * d + 8 * n * d * d, 14 << 20,
        out_specs=[a_block(k) for k in out_dims], grid=(blocks,),
    )
    pool = blocks + 8
    tile = (slots + 1, BLK, 2 * BLK)
    vmem = pltpu.VMEM
    ins = (pos, ids, cnt, gain, *arrived, w_query_key, w_value, *made, sc, n_t)
    ctx_t, dq_t, own, *back, keep, send, gain_term = call(
        functools.partial(attend_kernel, dims, np_), "attend",
        [shape((blocks, d, BLK), BF)] * 2 + [shape((blocks, 2, np_, BLK, PAIR), F32)]
        + [shape((2, 2, np_, BLK, PAIR), BF)] * 4
        + [shape((n, d), BF), shape((n + 16, d), BF), shape((8, d), F32)],
        ins, [SM] * 3 + [VM] + [AN] * (len(ins) - 4),
        [vmem((4, 2 * BLK, d), BF), vmem((d, 2 * d), BF), vmem((d, d), BF)]
        + [vmem(nat, BF), vmem(tra, BF)] * 2
        + [vmem((pool,) + nat[1:], BF), vmem((pool,) + tra[1:], BF)] * 2
        + [vmem((blocks, BLK, d), BF), vmem((pool, d, BLK), BF)] + [vmem((blocks, d, BLK), BF)] * 2
        + [vmem((pool, 2) + nat[1:], F32), vmem(tile, F32), vmem(tile, F32), vmem(tile, BF), vmem(tile, BF),
           vmem((2, n + 16, d), BF), pltpu.SMEM((blocks * slots,), jnp.int32),
           pltpu.SemaphoreType.DMA((16,)), pltpu.SemaphoreType.DMA((13,))],
        LIMIT, 12 * blocks * 5 * BLK * BLK * d, 24 << 20, blocks * 5 * BLK * BLK * 8,
        out_specs=[AN] * 9 + [VM],
    )
    h0, h1, h2, h3 = back
    cores = lax.ppermute(send, "by", [(i, i ^ 1) for i in range(extent_y)])
    returned = [
        step_to(h0, "bx", -1), step_to(h1, "bx", 1), step_to(h2, "by", -1), step_to(h3, "by", 1),
    ]
    mine, *cut, gain_sum = call(
        core_kernel, "add_cores",
        [shape((BLK, d), F32)] + [shape((BLK + 16, d), BF)] * 3 + [shape((8, d), F32)],
        (pos, keep, cores, gain_term), [SM, VM, VM, VM], [], 32, 0, 4 << 20,
    )
    count = extent_y // 2
    got = [
        lax.ppermute(cut[s - 1], "by", [(i, (i + 2 * s) % extent_y) for i in range(extent_y)])
        for s in range(1, count)
    ]
    branch_out, part = call(
        output_kernel, "branch_rows", [shape((n, d), BF), shape((n, d), F32)],
        (order, w_query_key, w_out, ctx_t, dq_t), [VM] * 5, [], 40,
        4 * n * n * d + 4 * n * d * d, 7 << 20,
    )
    rows, gain_sum = mine, gain_sum[:1]
    for g in got:
        rows = rows + g[:BLK].astype(F32)
        gain_sum = gain_sum + g[BLK : BLK + 1].astype(F32)
    rows, gain_sum, part, branch_out, *returned = lax.optimization_barrier(
        (rows, gain_sum, part, branch_out, *returned)
    )
    rows, gain_sum = across_x(rows, gain_sum)
    rows, part = lax.optimization_barrier((rows, part))
    rows = lax.all_gather(rows, "by", axis=0, tiled=True)

    b_x1, b_xm, b_y1, b_ym = returned
    grad_rows = call(
        functools.partial(rows_kernel, dims, np_), "token_rows", shape((n, d), F32),
        (pos, ids, cnt, order, tok, gain, w_query_key, w_value, part, own, b_x1, b_xm, b_y1, b_ym),
        [SM] * 3 + [VM] * 11,
        [pltpu.VMEM((blocks, 2, np_, BLK, PAIR), F32), pltpu.VMEM((n, 2 * d), BF)],
        56, 4 * n * n * d + 4 * n * d * d, 16 << 20,
    )
    grad_qk, grad_v, grad_o = call(
        place_kernel, "weight_grads", [shape((d, 2 * d), F32), shape((d, d), F32), shape((d, d), F32)],
        (rows,), [VM], [], 32, 0, 6 << 20,
    )
    return (branch_out[None, None], grad_rows[None, None], grad_qk, grad_v, grad_o, gain_sum[0])


def solution(mesh):
    local = P("bx", "by", None, None)
    placed = (local, P(), P(), P(), P(), local, P("bx", "by", None), P(), P())
    return jax.shard_map(
        shards,
        mesh=mesh,
        in_specs=placed,
        out_specs=(local, local, P(), P(), P(), P()),
        check_vma=False,
    )
```

```python
import functools

import jax
import jax.numpy as jnp
from jax import lax
from jax.experimental import pallas as pl
from jax.experimental.pallas import tpu as pltpu
from jax.sharding import PartitionSpec as P

BLK = 256
PAIR = 128
EPSILON = 1e-06
BF = jnp.bfloat16
F32 = jnp.float32
MIB = 1 << 20
LIMIT = 58
VM = pl.BlockSpec(memory_space=pltpu.VMEM)
SM = pl.BlockSpec(memory_space=pltpu.SMEM)
AN = pl.BlockSpec(memory_space=pl.ANY)
NT = (((1,), (1,)), ((), ()))


def mm(a, b):
    return jnp.dot(a, b, preferred_element_type=F32)


def mm_nt(a, b):
    return lax.dot_general(a, b, NT, preferred_element_type=F32)


def rms(rows):
    values = rows.astype(F32)
    inv = lax.rsqrt(jnp.mean(values * values, axis=-1, keepdims=True) + EPSILON)
    return values, inv


def named_mask(ids, cnt, reader, owner, blocks, slots):
    mask = jnp.int32(0)
    for b in range(blocks):
        count = cnt[reader * blocks + b]
        for j in range(slots):
            entry = ids[(reader * blocks + b) * slots + j]
            hit = jnp.logical_and(j < count, lax.div(entry, blocks) == owner)
            mask = mask | jnp.where(hit, jnp.left_shift(1, lax.rem(entry, blocks)), 0)
    return mask


def first_two(mask, blocks):
    def lowest(m):
        at = jnp.int32(blocks - 1)
        for b in range(blocks - 2, -1, -1):
            at = jnp.where((m & (1 << b)) != 0, b, at)
        return at

    first = lowest(mask)
    return first, lowest(mask & ~jnp.left_shift(1, first))


def send_table(ids, cnt, pos, extent_x, extent_y, blocks, slots):
    x, y = pos[0], pos[1]
    me = x * extent_y + y
    readers = (
        jnp.minimum(x + 1, extent_x - 1) * extent_y + y,
        jnp.maximum(x - 1, 0) * extent_y + y,
        x * extent_y + jnp.minimum(y + 1, extent_y - 1),
        x * extent_y + jnp.maximum(y - 1, 0),
    )
    return [first_two(named_mask(ids, cnt, r, me, blocks, slots), blocks) for r in readers]


def pool_table(ids, cnt, pos, extent_y, blocks, slots):
    me = pos[0] * extent_y + pos[1]
    owners = (me - extent_y, me + extent_y, me - 1, me + 1)
    masks = [named_mask(ids, cnt, me, o, blocks, slots) for o in owners]
    table = []
    for b in range(blocks):
        row = []
        for j in range(slots):
            entry = ids[(me * blocks + b) * slots + j]
            owner, off = lax.div(entry, blocks), lax.rem(entry, blocks)
            at = off
            for seg, (o, mask) in enumerate(zip(owners, masks)):
                below = mask & (jnp.left_shift(1, off) - 1)
                at = jnp.where(owner == o, blocks + 2 * seg + jnp.where(below != 0, 1, 0), at)
            live = j < cnt[me * blocks + b]
            row.append((jnp.where(live, at, b), live))
        table.append(row)
    return table


def order_columns(order_ref):
    n = order_ref.shape[1]
    return jnp.broadcast_to(order_ref[...], (128, n)).T


def one_hot_rows(cols, n):
    lane = lax.broadcasted_iota(jnp.int32, cols.shape, 1)
    return jnp.concatenate(
        [(cols == lane + c).astype(F32).astype(BF) for c in range(0, n, 128)], axis=1
    )


def one_hot_back(order_ref, start, rows):
    n = order_ref.shape[1]
    row = lax.broadcasted_iota(jnp.int32, (rows, n), 0) + start
    return (row == order_ref[...]).astype(F32).astype(BF)


def sort_kernel(dims, pos, ids, cnt, order, tok_in, out, s0, s1, s2, s3, cols, tok, sem):
    extent_x, extent_y, blocks, slots = dims
    n = tok.shape[0]
    copy = pltpu.make_async_copy(tok_in, tok, sem.at[0])
    copy.start()
    cols[...] = order_columns(order)
    table = send_table(ids, cnt, pos, extent_x, extent_y, blocks, slots)
    copy.wait()

    def body(b, _):
        rows = pl.ds(pl.multiple_of(b * BLK, BLK), BLK)
        out[rows, :] = mm(one_hot_rows(cols[rows, :], n), tok[...]).astype(BF)
        return 0

    lax.fori_loop(0, n // BLK, body, 0)
    for ref, pair in zip((s0, s1, s2, s3), table):
        for k, b in enumerate(pair):
            ref[k * BLK : (k + 1) * BLK, :] = out[pl.ds(pl.multiple_of(b * BLK, BLK), BLK), :]


def project_kernel(np_, order, tok, cot, gain, w_qk, w_v, w_out, sc, n_t, *rest):
    *outs, cols = rest
    n, d = cot.shape
    b = pl.program_id(0)

    @pl.when(b == 0)
    def _():
        cols[...] = order_columns(order)

    rows = pl.ds(pl.multiple_of(b * BLK, BLK), BLK)
    grad = mm(one_hot_rows(cols[rows, :], n), cot[...]).astype(BF)
    sc[...] = grad
    values, inv = rms(tok[...])
    normed = (values * inv * gain[...]).astype(BF)
    n_t[0] = normed.T
    query = (mm(normed, w_qk[:, :d]).astype(BF)) * BF(0.125)
    key = mm(normed, w_qk[:, d:]).astype(BF)
    value = mm(normed, w_v[...]).astype(BF)
    dctx = mm_nt(grad, w_out[...]).astype(BF)
    for at, mat in enumerate((query, key, value, dctx)):
        mat_t = mat.T
        for p in range(np_):
            outs[2 * at][0, p] = mat[:, p * PAIR : (p + 1) * PAIR]
            outs[2 * at + 1][0, p] = mat_t[p * PAIR : (p + 1) * PAIR, :]


def attend_kernel(dims, np_, pos, ids, cnt, gain, r0, r1, r2, r3, w_qk_in, w_v_in,
                  qn_in, qt_in, kn_in, kt_in, vn_in, vt_in, gn_in, gt_in, sc_in, nt_in,
                  ctx_out, dq_out, own, h0, h1, h2, h3, keep, send, gain_out,
                  far, w_qk, w_v, qn, qt, gn, gt, pkn, pkt, pvn, pvt, sc, n_t, ctx_t, dq_t, acc,
                  s_scr, dp_scr, p_scr, ds_scr, terms, where_ref, sem_in, sem_out):
    extent_x, extent_y, blocks, slots = dims
    d = w_v.shape[0]
    mine = pl.ds(0, blocks)
    first, later = [], []

    def fetch(src, dst, into):
        copy = pltpu.make_async_copy(src, dst, sem_in.at[len(first) + len(later)])
        copy.start()
        into.append(copy)

    fetch(w_qk_in, w_qk, first)
    fetch(w_v_in, w_v, first)
    for seg, ref in enumerate((r0, r1, r2, r3)):
        fetch(ref, far.at[seg], first)
    for src, dst in ((kn_in, pkn.at[mine]), (kt_in, pkt.at[mine]), (vn_in, pvn.at[mine]),
                     (vt_in, pvt.at[mine]), (qt_in, qt), (gt_in, gt), (qn_in, qn), (gn_in, gn),
                     (sc_in, sc)):
        fetch(src, dst, later)
    for b in range(blocks):
        fetch(nt_in.at[b], n_t.at[:, pl.ds(b * BLK, BLK)], later)
    table = pool_table(ids, cnt, pos, extent_y, blocks, slots)
    for b in range(blocks):
        for j in range(slots):
            where_ref[b * slots + j] = table[b][j][0]
    acc[...] = jnp.zeros_like(acc)
    for copy in first:
        copy.wait()

    def remote(i, _):
        rows = pl.ds(pl.multiple_of(lax.rem(i, 2) * BLK, BLK), BLK)
        values, inv = rms(far[lax.div(i, 2), rows, :])
        normed = (values * inv * gain[...]).astype(BF)
        n_t[:, pl.ds(pl.multiple_of((blocks + i) * BLK, BLK), BLK)] = normed.T
        made = mm(normed, w_qk[:, d:]).astype(BF)
        made_v = mm(normed, w_v[...]).astype(BF)
        for mat, nat, tra in ((made, pkn, pkt), (made_v, pvn, pvt)):
            mat_t = mat.T
            for p in range(np_):
                nat[blocks + i, p] = mat[:, p * PAIR : (p + 1) * PAIR]
                tra[blocks + i, p] = mat_t[p * PAIR : (p + 1) * PAIR, :]
        return 0

    lax.fori_loop(0, 8, remote, 0)
    for copy in later:
        copy.wait()
    lane = lax.broadcasted_iota(jnp.int32, (1, PAIR), 1)
    low_lanes = (lane < PAIR // 2).astype(F32).astype(BF)
    high_lanes = (lane >= PAIR // 2).astype(F32).astype(BF)
    half = PAIR // 2

    def diagonal(mat):
        zero = jnp.zeros((half, BLK), BF)
        return jnp.concatenate(
            [jnp.concatenate([mat[:half], zero], axis=1), jnp.concatenate([zero, mat[half:]], axis=1)],
            axis=0,
        )

    def pair(b, p, at):
        q_diag, g_diag = diagonal(qt[b, p]), diagonal(gt[b, p])
        top = None
        for j, k in enumerate(at):
            s = mm(pkn[k, p], q_diag)
            s_scr[j] = s
            m = jnp.max(s, axis=0, keepdims=True)
            top = m if top is None else jnp.maximum(top, m)
        total = jnp.zeros((1, 2 * BLK), F32)
        centre = jnp.zeros((1, 2 * BLK), F32)
        for j, k in enumerate(at):
            e = jnp.exp(s_scr[j] - top)
            s_scr[j] = e
            total += jnp.sum(e, axis=0, keepdims=True)
            dp = mm(pvn[k, p], g_diag)
            dp_scr[j] = dp
            centre += jnp.sum(e * dp, axis=0, keepdims=True)
        scale = 1.0 / total
        centre = centre * scale
        for j in range(len(at)):
            prob = s_scr[j] * scale
            p_scr[j] = prob.astype(BF)
            ds_scr[j] = (prob * (dp_scr[j] - centre)).astype(BF)
        q_rows = qn[b, p]
        g_rows = gn[b, p]
        q_mask = jnp.concatenate([q_rows * low_lanes, q_rows * high_lanes], axis=0)
        g_mask = jnp.concatenate([g_rows * low_lanes, g_rows * high_lanes], axis=0)
        for h in range(2):
            feats, lanes = slice(h * half, (h + 1) * half), slice(h * BLK, (h + 1) * BLK)
            ctx = dq = None
            for j, k in enumerate(at):
                c = mm(pvt[k, p, feats, :], p_scr[j, :, lanes])
                t = mm(pkt[k, p, feats, :], ds_scr[j, :, lanes])
                ctx = c if ctx is None else ctx + c
                dq = t if dq is None else dq + t
            rows = pl.ds(pl.multiple_of(p * PAIR + h * half, half), half)
            cols = pl.ds(pl.multiple_of(b * BLK, BLK), BLK)
            ctx_t[rows, cols] = ctx.astype(BF)
            dq_t[rows, cols] = (dq * 0.125).astype(BF)
        for j, k in enumerate(at):
            acc[k, 0, p] += mm(ds_scr[j], q_mask)
            acc[k, 1, p] += mm(p_scr[j], g_mask)

    me = pos[0] * extent_y + pos[1]

    def block(b, _):
        count = cnt[me * blocks + b]
        for live in range(1, slots + 1):

            @pl.when(count == live)
            def _():
                at = [b] + [where_ref[b * slots + j] for j in range(live)]
                lax.fori_loop(0, np_, lambda p, c: (pair(b, p, at), c)[1], 0)

        return 0

    lax.fori_loop(0, blocks, block, 0)
    out = []

    def ship(src, dst):
        copy = pltpu.make_async_copy(src, dst, sem_out.at[len(out)])
        copy.start()
        out.append(copy)

    ship(ctx_t, ctx_out)
    ship(dq_t, dq_out)
    ship(acc.at[mine], own)

    def lower(b, _):
        for p in range(np_):
            pkn[b, p] = acc[b, 0, p].astype(BF)
            pvn[b, p] = acc[b, 1, p].astype(BF)
        return 0

    lax.fori_loop(0, blocks + 8, lower, 0)
    for seg, ref in enumerate((h0, h1, h2, h3)):
        part = pl.ds(blocks + 2 * seg, 2)
        ship(pkn.at[part], ref.at[0])
        ship(pvn.at[part], ref.at[1])
    core = lax.rem(pos[1], 2)
    total = jnp.zeros((d, 1), F32)

    def place(i, value):
        terms[lax.rem(i + core, 2), (i // 2) * BLK : (i // 2 + 1) * BLK, :] = value.astype(BF)

    g_q = mm_nt(n_t[:, : blocks * BLK], dq_t[...])
    g_o = mm(ctx_t[...], sc[...])
    for i, g in ((0, g_q), (6, g_o)):
        place(i, g[:BLK])
        place(i + 1, g[BLK:])
    total += jnp.sum(g_q * w_qk[:, :d].astype(F32), axis=1, keepdims=True)
    for i, pool, w, lo in ((2, pkn, w_qk, d), (4, pvn, w_v, 0)):
        made = []
        for p in range(0, np_, 2):
            cols = [jnp.concatenate([pool[b, p], pool[b, p + 1]], axis=1) for b in range(blocks + 8)]
            g = mm(n_t[...], jnp.concatenate(cols, axis=0))
            at = lo + p * PAIR
            total += jnp.sum(g * w[:, at : at + 2 * PAIR].astype(F32), axis=1, keepdims=True)
            made.append(g)
        g = jnp.concatenate(made, axis=1)
        place(i, g[:BLK])
        place(i + 1, g[BLK:])
    gain_term = jnp.broadcast_to(total, (d, 128)).T[:8] / gain[...]
    gain_out[...] = gain_term
    terms[:, blocks * BLK :, :] = jnp.broadcast_to(gain_term[:1].astype(BF)[None], (2, 16, d))
    ship(terms.at[0, pl.ds(0, blocks * BLK)], keep)
    ship(terms.at[1], send)
    for copy in out:
        copy.wait()


def core_kernel(pos, keep, got, gain, own, s1, s2, s3, gain_out):
    size, d = own.shape
    rows = 4 * size
    total = gain[:1] + got[rows : rows + 1, :].astype(F32)
    gain_out[...] = jnp.broadcast_to(total, gain_out.shape)
    y = lax.div(pos[1], 2)
    for s, ref in enumerate((own, s1, s2, s3)):
        at = pl.ds(pl.multiple_of(lax.rem(y + s, 4) * size, size), size)
        value = keep[at, :].astype(F32) + got[at, :].astype(F32)
        if s:
            ref[:size, :] = value.astype(BF)
            ref[size:, :] = jnp.broadcast_to(total, (ref.shape[0] - size, d)).astype(BF)
        else:
            ref[...] = value


def output_kernel(order, w_qk, w_out, ctx_t, dq_t, out, part):
    d = w_out.shape[0]

    def body(a, _):
        rows = pl.ds(pl.multiple_of(a * BLK, BLK), BLK)
        back = one_hot_back(order, a * BLK, BLK)
        ctx = mm_nt(back, ctx_t[...]).astype(BF)
        dq = mm_nt(back, dq_t[...]).astype(BF)
        out[rows, :] = mm(ctx, w_out[...]).astype(BF)
        part[rows, :] = mm_nt(dq, w_qk[:, :d])
        return 0

    lax.fori_loop(0, out.shape[0] // BLK, body, 0)


def rows_kernel(dims, np_, pos, ids, cnt, order, tok, gain, w_qk, w_v, part, own, b0, b1, b2, b3,
                out, acc, rows_scr):
    extent_x, extent_y, blocks, slots = dims
    d = w_v.shape[0]
    acc[...] = own[...]
    table = send_table(ids, cnt, pos, extent_x, extent_y, blocks, slots)
    for ref, pair in zip((b0, b1, b2, b3), table):
        for k, b in enumerate(pair):
            acc[b, 0] += ref[0, k].astype(F32)
            acc[b, 1] += ref[1, k].astype(F32)
    for half in range(2):
        for p in range(np_):
            lo = half * d + p * PAIR
            for b in range(blocks):
                rows_scr[b * BLK : (b + 1) * BLK, lo : lo + PAIR] = acc[b, half, p].astype(BF)

    def body(a, _):
        rows = pl.ds(pl.multiple_of(a * BLK, BLK), BLK)
        back = one_hot_back(order, a * BLK, BLK)
        mine = mm(back, rows_scr[...]).astype(BF)
        grad = part[rows, :] + mm_nt(mine[:, :d], w_qk[:, d:]) + mm_nt(mine[:, d:], w_v[...])
        values, inv = rms(tok[rows, :])
        u = grad * gain[...]
        mean = jnp.mean(values * u, axis=-1, keepdims=True)
        out[rows, :] = inv * u - values * (inv * inv * inv * mean)
        return 0

    lax.fori_loop(0, out.shape[0] // BLK, body, 0)


def place_kernel(pos, *refs):
    *parts, qk, v, o, rows = refs
    d = v.shape[0]
    count = len(parts) // 2
    core, y = lax.rem(pos[1], 2), lax.div(pos[1], 2)
    size = parts[0].shape[0]
    for i, ref in enumerate(parts):
        c = core if i < count else 1 - core
        at = (lax.rem(y - i % count + count, count) * 2 + c) * size
        rows[pl.ds(pl.multiple_of(at, size), size), :] = ref[...]
    qk[:, :d] = rows[:d, :].astype(F32)
    qk[:, d:] = rows[d : 2 * d, :].astype(F32)
    v[...] = rows[2 * d : 3 * d, :].astype(F32)
    o[...] = rows[3 * d :, :].astype(F32)


def step_to(block, axis, distance):
    n = lax.axis_size(axis)
    route = [(i, i + distance) for i in range(n) if 0 <= i + distance < n]
    return lax.ppermute(block, axis, route)


def across_x(rows, gain):
    count = lax.axis_size("bx")
    size = rows.shape[0] // count
    extra = jnp.zeros((size, 128), F32).at[: gain.shape[1] // 128].set(gain.reshape(-1, 128))
    extra = jnp.broadcast_to(extra[None], (count, size, 128))
    parts = jnp.concatenate([rows.reshape(count, size, -1), extra], axis=2).astype(BF)
    got = lax.all_to_all(parts, "bx", 0, 0, tiled=True)
    total = jnp.sum(got.astype(F32), axis=0)
    gain = total[: gain.shape[1] // 128, rows.shape[1] :].reshape(1, -1)
    mine = total[:, : rows.shape[1]].astype(BF)
    back = lax.all_to_all(jnp.broadcast_to(mine[None], (count,) + mine.shape), "bx", 0, 0, tiled=True)
    return back.reshape(rows.shape), gain


def call(kernel, name, outs, ins, specs, scratch, limit, flops, moved, exps=0, out_specs=None, grid=()):
    return pl.pallas_call(
        kernel,
        out_shape=outs,
        grid=grid,
        in_specs=specs,
        out_specs=jax.tree.map(lambda _: VM, outs) if out_specs is None else out_specs,
        scratch_shapes=scratch,
        compiler_params=pltpu.CompilerParams(vmem_limit_bytes=limit * MIB),
        cost_estimate=pl.CostEstimate(flops=flops, bytes_accessed=moved, transcendentals=exps),
        name=name,
    )(*ins)


def shards(tokens, norm_gain, w_query_key, w_value, w_out, cotangent, block_order,
           neighbour_ids, neighbour_count):
    n, d = tokens.shape[2:]
    extent_x, extent_y, blocks, slots = neighbour_ids.shape
    dims = (extent_x, extent_y, blocks, slots)
    np_ = d // PAIR
    tok, cot = tokens[0, 0], cotangent[0, 0]
    order = block_order[0]
    gain = norm_gain[None, :]
    ids = neighbour_ids.reshape(-1)
    cnt = neighbour_count.reshape(-1)
    pos = jnp.stack([lax.axis_index("bx"), lax.axis_index("by")]).astype(jnp.int32)
    shape = jax.ShapeDtypeStruct

    sends = [shape((2 * BLK, d), BF)] * 4
    sorted_rows, *sent = call(
        functools.partial(sort_kernel, dims), "sort_rows",
        [shape((n, d), BF)] + sends, (pos, ids, cnt, order, tok), [SM, SM, SM, VM, AN],
        [pltpu.VMEM((n, 128), jnp.int32), pltpu.VMEM((n, d), BF), pltpu.SemaphoreType.DMA((1,))], 32, 2 * n * n * d, 4 << 20,
    )
    arrived = [
        step_to(sent[0], "bx", 1), step_to(sent[1], "bx", -1),
        step_to(sent[2], "by", 1), step_to(sent[3], "by", -1),
    ]
    nat, tra = (blocks, np_, BLK, PAIR), (blocks, np_, PAIR, BLK)

    def a_block(dims_):
        return pl.BlockSpec((1,) + dims_[1:], lambda b: (b,) + (0,) * (len(dims_) - 1))

    whole = pl.BlockSpec(memory_space=pltpu.VMEM)
    out_dims = [(n, d), (blocks, d, BLK)] + [nat, tra] * 4
    sc, n_t, *made = call(
        functools.partial(project_kernel, np_), "project", [shape(k, BF) for k in out_dims],
        (order, sorted_rows, cot, gain, w_query_key, w_value, w_out),
        [whole, pl.BlockSpec((BLK, d), lambda b: (b, 0))] + [whole] * 5,
        [pltpu.VMEM((n, 128), jnp.int32)], LIMIT, 2 * n * n * d + 8 * n * d * d, 14 << 20,
        out_specs=[pl.BlockSpec((BLK, d), lambda b: (b, 0))] + [a_block(k) for k in out_dims[1:]], grid=(blocks,),
    )
    pool = blocks + 8
    tile = (slots + 1, BLK, 2 * BLK)
    vmem = pltpu.VMEM
    ins = (pos, ids, cnt, gain, *arrived, w_query_key, w_value, *made, sc, n_t)
    ctx_t, dq_t, own, *back, keep, send, gain_term = call(
        functools.partial(attend_kernel, dims, np_), "attend",
        [shape((d, n), BF)] * 2 + [shape((blocks, 2, np_, BLK, PAIR), F32)]
        + [shape((2, 2, np_, BLK, PAIR), BF)] * 4
        + [shape((n, d), BF), shape((n + 16, d), BF), shape((8, d), F32)],
        ins, [SM] * 3 + [VM] + [AN] * (len(ins) - 4),
        [vmem((4, 2 * BLK, d), BF), vmem((d, 2 * d), BF), vmem((d, d), BF)]
        + [vmem(nat, BF), vmem(tra, BF)] * 2
        + [vmem((pool,) + nat[1:], BF), vmem((pool,) + tra[1:], BF)] * 2
        + [vmem((n, d), BF), vmem((d, pool * BLK), BF)] + [vmem((d, n), BF)] * 2
        + [vmem((pool, 2) + nat[1:], F32), vmem(tile, F32), vmem(tile, F32), vmem(tile, BF), vmem(tile, BF),
           vmem((2, n + 16, d), BF), pltpu.SMEM((blocks * slots,), jnp.int32),
           pltpu.SemaphoreType.DMA((20,)), pltpu.SemaphoreType.DMA((13,))],
        LIMIT, 12 * blocks * 5 * BLK * BLK * d, 24 << 20, blocks * 5 * BLK * BLK * 8,
        out_specs=[AN] * 9 + [VM],
    )
    h0, h1, h2, h3 = back
    cores = lax.ppermute(send, "by", [(i, i ^ 1) for i in range(extent_y)])
    b_x = [step_to(h0, "bx", -1), step_to(h1, "bx", 1)]
    mine, *cut, gain_sum = call(
        core_kernel, "add_cores",
        [shape((BLK, d), F32)] + [shape((BLK + 16, d), BF)] * 3 + [shape((8, d), F32)],
        (pos, keep, cores, gain_term), [SM, VM, VM, VM], [], 32, 0, 4 << 20,
    )
    count = extent_y // 2

    def along_y(rows, s):
        return lax.ppermute(rows, "by", [(i, (i + 2 * s) % extent_y) for i in range(extent_y)])

    def other_core(rows):
        return lax.ppermute(rows, "by", [(i, i ^ 1) for i in range(extent_y)])

    got = [along_y(cut[s - 1], s) for s in range(1, count)]
    branch_out, part = call(
        output_kernel, "branch_rows", [shape((n, d), BF), shape((n, d), F32)],
        (order, w_query_key, w_out, ctx_t, dq_t), [VM] * 5, [], 40,
        4 * n * n * d + 4 * n * d * d, 7 << 20,
    )
    got, h2, h3 = lax.optimization_barrier((got, h2, h3))
    b_y = [step_to(h2, "by", -1), step_to(h3, "by", 1)]
    rows, gain_sum = mine, gain_sum[:1]
    for g in got:
        rows = rows + g[:BLK].astype(F32)
        gain_sum = gain_sum + g[BLK : BLK + 1].astype(F32)
    rows, gain_sum, part, branch_out, b_x = lax.optimization_barrier((rows, gain_sum, part, branch_out, b_x))
    rows, gain_sum = across_x(rows, gain_sum)
    rows, part = lax.optimization_barrier((rows, part))
    chunks = [rows] + [along_y(rows, s) for s in range(1, count)]

    grad_rows = call(
        functools.partial(rows_kernel, dims, np_), "token_rows", shape((n, d), F32),
        (pos, ids, cnt, order, tok, gain, w_query_key, w_value, part, own, *b_x, *b_y),
        [SM] * 3 + [VM] * 11,
        [pltpu.VMEM((blocks, 2, np_, BLK, PAIR), F32), pltpu.VMEM((n, 2 * d), BF)],
        56, 4 * n * n * d + 4 * n * d * d, 16 << 20,
    )
    chunks, grad_rows = lax.optimization_barrier((chunks, grad_rows))
    chunks = chunks + [other_core(c) for c in chunks]
    grad_qk, grad_v, grad_o = call(
        place_kernel, "weight_grads", [shape((d, 2 * d), F32), shape((d, d), F32), shape((d, d), F32)],
        (pos, *chunks), [SM] + [VM] * 8, [pltpu.VMEM((4 * d, d), BF)], 32, 0, 6 << 20,
    )
    return (branch_out[None, None], grad_rows[None, None], grad_qk, grad_v, grad_o, gain_sum[0])


def solution(mesh):
    local = P("bx", "by", None, None)
    placed = (local, P(), P(), P(), P(), local, P("bx", "by", None), P(), P())
    return jax.shard_map(
        shards,
        mesh=mesh,
        in_specs=placed,
        out_specs=(local, local, P(), P(), P(), P()),
        check_vma=False,
    )
```

```python
import functools

import jax
import jax.numpy as jnp
from jax import lax
from jax.experimental import pallas as pl
from jax.experimental.pallas import tpu as pltpu
from jax.sharding import PartitionSpec as P

BLK = 256
PAIR = 128
EPSILON = 1e-06
BF = jnp.bfloat16
F32 = jnp.float32
MIB = 1 << 20
LIMIT = 58
WIDE = 512
VM = pl.BlockSpec(memory_space=pltpu.VMEM)
SM = pl.BlockSpec(memory_space=pltpu.SMEM)
AN = pl.BlockSpec(memory_space=pl.ANY)
NT = (((1,), (1,)), ((), ()))


def mm(a, b):
    return jnp.dot(a, b, preferred_element_type=F32)


def mm_nt(a, b):
    return lax.dot_general(a, b, NT, preferred_element_type=F32)


def rms(rows):
    values = rows.astype(F32)
    inv = lax.rsqrt(jnp.mean(values * values, axis=-1, keepdims=True) + EPSILON)
    return values, inv


def named_mask(ids, cnt, reader, owner, blocks, slots):
    mask = jnp.int32(0)
    for b in range(blocks):
        count = cnt[reader * blocks + b]
        for j in range(slots):
            entry = ids[(reader * blocks + b) * slots + j]
            hit = jnp.logical_and(j < count, lax.div(entry, blocks) == owner)
            mask = mask | jnp.where(hit, jnp.left_shift(1, lax.rem(entry, blocks)), 0)
    return mask


def first_two(mask, blocks):
    def lowest(m):
        at = jnp.int32(blocks - 1)
        for b in range(blocks - 2, -1, -1):
            at = jnp.where((m & (1 << b)) != 0, b, at)
        return at

    first = lowest(mask)
    return first, lowest(mask & ~jnp.left_shift(1, first))


def send_table(ids, cnt, pos, extent_x, extent_y, blocks, slots):
    x, y = pos[0], pos[1]
    me = x * extent_y + y
    readers = (
        jnp.minimum(x + 1, extent_x - 1) * extent_y + y,
        jnp.maximum(x - 1, 0) * extent_y + y,
        x * extent_y + jnp.minimum(y + 1, extent_y - 1),
        x * extent_y + jnp.maximum(y - 1, 0),
    )
    return [first_two(named_mask(ids, cnt, r, me, blocks, slots), blocks) for r in readers]


def pool_table(ids, cnt, pos, extent_y, blocks, slots):
    me = pos[0] * extent_y + pos[1]
    owners = (me - extent_y, me + extent_y, me - 1, me + 1)
    masks = [named_mask(ids, cnt, me, o, blocks, slots) for o in owners]
    table = []
    for b in range(blocks):
        row = []
        for j in range(slots):
            entry = ids[(me * blocks + b) * slots + j]
            owner, off = lax.div(entry, blocks), lax.rem(entry, blocks)
            at = off
            for seg, (o, mask) in enumerate(zip(owners, masks)):
                below = mask & (jnp.left_shift(1, off) - 1)
                at = jnp.where(owner == o, blocks + 2 * seg + jnp.where(below != 0, 1, 0), at)
            live = j < cnt[me * blocks + b]
            row.append((jnp.where(live, at, b), live))
        table.append(row)
    return table


def order_columns(order_ref):
    n = order_ref.shape[1]
    return jnp.broadcast_to(order_ref[...], (128, n)).T


def one_hot_rows(cols, n):
    lane = lax.broadcasted_iota(jnp.int32, cols.shape, 1)
    return jnp.concatenate(
        [(cols == lane + c).astype(F32).astype(BF) for c in range(0, n, 128)], axis=1
    )


def one_hot_back(order_ref, start, rows):
    n = order_ref.shape[1]
    row = lax.broadcasted_iota(jnp.int32, (rows, n), 0) + start
    return (row == order_ref[...]).astype(F32).astype(BF)


def sort_kernel(dims, pos, ids, cnt, order, tok_in, out, s0, s1, s2, s3, cols, tok, sem):
    extent_x, extent_y, blocks, slots = dims
    n = tok.shape[0]
    copy = pltpu.make_async_copy(tok_in, tok, sem.at[0])
    copy.start()
    cols[...] = order_columns(order)
    table = send_table(ids, cnt, pos, extent_x, extent_y, blocks, slots)
    copy.wait()

    def body(b, _):
        rows = pl.ds(pl.multiple_of(b * BLK, BLK), BLK)
        out[rows, :] = mm(one_hot_rows(cols[rows, :], n), tok[...]).astype(BF)
        return 0

    lax.fori_loop(0, n // BLK, body, 0)
    for ref, pair in zip((s0, s1, s2, s3), table):
        for k, b in enumerate(pair):
            ref[k * BLK : (k + 1) * BLK, :] = out[pl.ds(pl.multiple_of(b * BLK, BLK), BLK), :]


def project_kernel(np_, order, tok, cot, gain, w_qk, w_v, w_out, sc, n_t, *rest):
    *outs, cols = rest
    n, d = cot.shape
    b = pl.program_id(0)

    @pl.when(b == 0)
    def _():
        cols[...] = order_columns(order)

    rows = pl.ds(pl.multiple_of(b * BLK, BLK), BLK)
    grad = mm(one_hot_rows(cols[rows, :], n), cot[...]).astype(BF)
    sc[...] = grad
    values, inv = rms(tok[...])
    normed = (values * inv * gain[...]).astype(BF)
    n_t[0] = normed.T
    query = (mm(normed, w_qk[:, :d]).astype(BF)) * BF(0.125)
    key = mm(normed, w_qk[:, d:]).astype(BF)
    value = mm(normed, w_v[...]).astype(BF)
    dctx = mm_nt(grad, w_out[...]).astype(BF)
    for at, mat in enumerate((query, key, value, dctx)):
        mat_t = mat.T
        for p in range(np_):
            outs[2 * at][0, p] = mat[:, p * PAIR : (p + 1) * PAIR]
            outs[2 * at + 1][0, p] = mat_t[p * PAIR : (p + 1) * PAIR, :]


def attend_kernel(dims, np_, pos, ids, cnt, gain, r0, r1, r2, r3, w_qk_in, w_v_in,
                  qn_in, qt_in, kn_in, kt_in, vn_in, vt_in, gn_in, gt_in, sc_in, nt_in,
                  ctx_out, dq_out, own, h0, h1, h2, h3, keep, send, gain_out,
                  far, w_qk, w_v, qn, qt, gn, gt, pkn, pkt, pvn, pvt, sc, n_t, ctx_t, dq_t, acc,
                  s_scr, dp_scr, p_a, ds_a, p_b, ds_b, terms, where_ref, sem_in, sem_out):
    extent_x, extent_y, blocks, slots = dims
    d = w_v.shape[0]
    mine = pl.ds(0, blocks)
    scratch = ((p_a, ds_a), (p_b, ds_b))
    first, later = [], []

    def fetch(src, dst, into):
        copy = pltpu.make_async_copy(src, dst, sem_in.at[len(first) + len(later)])
        copy.start()
        into.append(copy)

    fetch(w_qk_in, w_qk, first)
    fetch(w_v_in, w_v, first)
    for seg, ref in enumerate((r0, r1, r2, r3)):
        fetch(ref, far.at[seg], first)
    for src, dst in ((kn_in, pkn.at[mine]), (kt_in, pkt.at[mine]), (vn_in, pvn.at[mine]),
                     (vt_in, pvt.at[mine]), (qt_in, qt), (gt_in, gt), (qn_in, qn), (gn_in, gn),
                     (sc_in, sc)):
        fetch(src, dst, later)
    for b in range(blocks):
        fetch(nt_in.at[b], n_t.at[:, pl.ds(b * BLK, BLK)], later)
    table = pool_table(ids, cnt, pos, extent_y, blocks, slots)
    for b in range(blocks):
        for j in range(slots):
            where_ref[b * slots + j] = table[b][j][0]
    acc[...] = jnp.zeros_like(acc)
    for copy in first:
        copy.wait()

    def remote(i, _):
        rows = pl.ds(pl.multiple_of(lax.rem(i, 2) * BLK, BLK), BLK)
        values, inv = rms(far[lax.div(i, 2), rows, :])
        normed = (values * inv * gain[...]).astype(BF)
        n_t[:, pl.ds(pl.multiple_of((blocks + i) * BLK, BLK), BLK)] = normed.T
        made = mm(normed, w_qk[:, d:]).astype(BF)
        made_v = mm(normed, w_v[...]).astype(BF)
        for mat, nat, tra in ((made, pkn, pkt), (made_v, pvn, pvt)):
            mat_t = mat.T
            for p in range(np_):
                nat[blocks + i, p] = mat[:, p * PAIR : (p + 1) * PAIR]
                tra[blocks + i, p] = mat_t[p * PAIR : (p + 1) * PAIR, :]
        return 0

    lax.fori_loop(0, 8, remote, 0, unroll=2)
    for copy in later:
        copy.wait()
    lane = lax.broadcasted_iota(jnp.int32, (1, PAIR), 1)
    low_lanes = (lane < PAIR // 2).astype(F32).astype(BF)
    high_lanes = (lane >= PAIR // 2).astype(F32).astype(BF)
    half = PAIR // 2

    def diagonal(mat):
        zero = jnp.zeros((half, BLK), BF)
        return jnp.concatenate(
            [jnp.concatenate([mat[:half], zero], axis=1), jnp.concatenate([zero, mat[half:]], axis=1)],
            axis=0,
        )

    def weigh(b, p, at, p_scr, ds_scr):
        q_diag, g_diag = diagonal(qt[b, p]), diagonal(gt[b, p])
        top = None
        for j, k in enumerate(at):
            s = mm(pkn[k, p], q_diag)
            s_scr[j] = s
            m = jnp.max(s, axis=0, keepdims=True)
            top = m if top is None else jnp.maximum(top, m)
        total = jnp.zeros((1, 2 * BLK), F32)
        centre = jnp.zeros((1, 2 * BLK), F32)
        for j, k in enumerate(at):
            e = jnp.exp(s_scr[j] - top)
            s_scr[j] = e
            total += jnp.sum(e, axis=0, keepdims=True)
            dp = mm(pvn[k, p], g_diag)
            dp_scr[j] = dp
            centre += jnp.sum(e * dp, axis=0, keepdims=True)
        scale = 1.0 / total
        centre = centre * scale
        for j in range(len(at)):
            prob = s_scr[j] * scale
            p_scr[j] = prob.astype(BF)
            ds_scr[j] = (prob * (dp_scr[j] - centre)).astype(BF)

    def spread(b, p, at, p_scr, ds_scr):
        q_rows = qn[b, p]
        g_rows = gn[b, p]
        q_mask = jnp.concatenate([q_rows * low_lanes, q_rows * high_lanes], axis=0)
        g_mask = jnp.concatenate([g_rows * low_lanes, g_rows * high_lanes], axis=0)
        for h in range(2):
            feats, lanes = slice(h * half, (h + 1) * half), slice(h * BLK, (h + 1) * BLK)
            ctx = dq = None
            for j, k in enumerate(at):
                c = mm(pvt[k, p, feats, :], p_scr[j, :, lanes])
                t = mm(pkt[k, p, feats, :], ds_scr[j, :, lanes])
                ctx = c if ctx is None else ctx + c
                dq = t if dq is None else dq + t
            rows = pl.ds(pl.multiple_of(p * PAIR + h * half, half), half)
            cols = pl.ds(pl.multiple_of(b * BLK, BLK), BLK)
            ctx_t[rows, cols] = ctx.astype(BF)
            dq_t[rows, cols] = (dq * 0.125).astype(BF)
        for j, k in enumerate(at):
            acc[k, 0, p] += mm(ds_scr[j], q_mask)
            acc[k, 1, p] += mm(p_scr[j], g_mask)

    me = pos[0] * extent_y + pos[1]

    def block(b, _):
        count = cnt[me * blocks + b]
        for live in range(1, slots + 1):

            @pl.when(count == live)
            def _():
                at = [b] + [where_ref[b * slots + j] for j in range(live)]

                def two(i, c):
                    for k, scr in enumerate(scratch):
                        weigh(b, 2 * i + k, at, *scr)
                    for k, scr in enumerate(scratch):
                        spread(b, 2 * i + k, at, *scr)
                    return c

                lax.fori_loop(0, np_ // 2, two, 0)

        return 0

    lax.fori_loop(0, blocks, block, 0)
    out = []

    def ship(src, dst):
        copy = pltpu.make_async_copy(src, dst, sem_out.at[len(out)])
        copy.start()
        out.append(copy)

    ship(ctx_t, ctx_out)
    ship(dq_t, dq_out)
    ship(acc.at[mine], own)

    def lower(b, _):
        for p in range(np_):
            pkn[b, p] = acc[b, 0, p].astype(BF)
            pvn[b, p] = acc[b, 1, p].astype(BF)
        return 0

    lax.fori_loop(0, blocks + 8, lower, 0)
    for seg, ref in enumerate((h0, h1, h2, h3)):
        part = pl.ds(blocks + 2 * seg, 2)
        ship(pkn.at[part], ref.at[0])
        ship(pvn.at[part], ref.at[1])
    core = lax.rem(pos[1], 2)
    total = jnp.zeros((d, 1), F32)

    def place(i, value):
        terms[lax.rem(i + core, 2), (i // 2) * BLK : (i // 2 + 1) * BLK, :] = value.astype(BF)

    g_q = mm_nt(n_t[:, : blocks * BLK], dq_t[...])
    g_o = mm(ctx_t[...], sc[...])
    for i, g in ((0, g_q), (6, g_o)):
        place(i, g[:BLK])
        place(i + 1, g[BLK:])
    total += jnp.sum(g_q * w_qk[:, :d].astype(F32), axis=1, keepdims=True)
    for i, pool, w, lo in ((2, pkn, w_qk, d), (4, pvn, w_v, 0)):
        made = []
        for p in range(0, np_, 2):
            cols = [jnp.concatenate([pool[b, p], pool[b, p + 1]], axis=1) for b in range(blocks + 8)]
            g = mm(n_t[...], jnp.concatenate(cols, axis=0))
            at = lo + p * PAIR
            total += jnp.sum(g * w[:, at : at + 2 * PAIR].astype(F32), axis=1, keepdims=True)
            made.append(g)
        g = jnp.concatenate(made, axis=1)
        place(i, g[:BLK])
        place(i + 1, g[BLK:])
    gain_term = jnp.broadcast_to(total, (d, 128)).T[:8] / gain[...]
    gain_out[...] = gain_term
    terms[:, blocks * BLK :, :] = jnp.broadcast_to(gain_term[:1].astype(BF)[None], (2, 16, d))
    ship(terms.at[0, pl.ds(0, blocks * BLK)], keep)
    ship(terms.at[1], send)
    for copy in out:
        copy.wait()


def core_kernel(pos, keep, got, gain, own, s1, s2, s3, gain_out):
    size, d = own.shape
    rows = 4 * size
    total = gain[:1] + got[rows : rows + 1, :].astype(F32)
    gain_out[...] = jnp.broadcast_to(total, gain_out.shape)
    y = lax.div(pos[1], 2)
    for s, ref in enumerate((own, s1, s2, s3)):
        at = pl.ds(pl.multiple_of(lax.rem(y + s, 4) * size, size), size)
        value = keep[at, :].astype(F32) + got[at, :].astype(F32)
        if s:
            ref[:size, :] = value.astype(BF)
            ref[size:, :] = jnp.broadcast_to(total, (ref.shape[0] - size, d)).astype(BF)
        else:
            ref[...] = value


def output_kernel(order, w_qk, w_out, ctx_t, dq_t, out, part):
    d = w_out.shape[0]

    def body(a, _):
        rows = pl.ds(pl.multiple_of(a * WIDE, WIDE), WIDE)
        back = one_hot_back(order, a * WIDE, WIDE)
        ctx = mm_nt(back, ctx_t[...]).astype(BF)
        dq = mm_nt(back, dq_t[...]).astype(BF)
        out[rows, :] = mm(ctx, w_out[...]).astype(BF)
        part[rows, :] = mm_nt(dq, w_qk[:, :d])
        return 0

    lax.fori_loop(0, out.shape[0] // WIDE, body, 0)


def rows_kernel(dims, np_, pos, ids, cnt, order, tok, gain, w_qk, w_v, part, own, b0, b1, b2, b3,
                out, acc, rows_scr):
    extent_x, extent_y, blocks, slots = dims
    d = w_v.shape[0]
    acc[...] = own[...]
    table = send_table(ids, cnt, pos, extent_x, extent_y, blocks, slots)
    for ref, pair in zip((b0, b1, b2, b3), table):
        for k, b in enumerate(pair):
            acc[b, 0] += ref[0, k].astype(F32)
            acc[b, 1] += ref[1, k].astype(F32)
    for half in range(2):
        for p in range(np_):
            lo = half * d + p * PAIR
            for b in range(blocks):
                rows_scr[b * BLK : (b + 1) * BLK, lo : lo + PAIR] = acc[b, half, p].astype(BF)

    def body(a, _):
        rows = pl.ds(pl.multiple_of(a * WIDE, WIDE), WIDE)
        back = one_hot_back(order, a * WIDE, WIDE)
        mine = mm(back, rows_scr[...]).astype(BF)
        grad = part[rows, :] + mm_nt(mine[:, :d], w_qk[:, d:]) + mm_nt(mine[:, d:], w_v[...])
        values, inv = rms(tok[rows, :])
        u = grad * gain[...]
        mean = jnp.mean(values * u, axis=-1, keepdims=True)
        out[rows, :] = inv * u - values * (inv * inv * inv * mean)
        return 0

    lax.fori_loop(0, out.shape[0] // WIDE, body, 0)


def place_kernel(pos, *refs):
    *parts, qk, v, o, rows = refs
    d = v.shape[0]
    count = len(parts) // 2
    core, y = lax.rem(pos[1], 2), lax.div(pos[1], 2)
    size = parts[0].shape[0]
    for i, ref in enumerate(parts):
        c = core if i < count else 1 - core
        at = (lax.rem(y - i % count + count, count) * 2 + c) * size
        rows[pl.ds(pl.multiple_of(at, size), size), :] = ref[...]
    qk[:, :d] = rows[:d, :].astype(F32)
    qk[:, d:] = rows[d : 2 * d, :].astype(F32)
    v[...] = rows[2 * d : 3 * d, :].astype(F32)
    o[...] = rows[3 * d :, :].astype(F32)


def step_to(block, axis, distance):
    n = lax.axis_size(axis)
    route = [(i, i + distance) for i in range(n) if 0 <= i + distance < n]
    return lax.ppermute(block, axis, route)


def across_x(rows, gain):
    count = lax.axis_size("bx")
    size = rows.shape[0] // count
    extra = jnp.zeros((size, 128), F32).at[: gain.shape[1] // 128].set(gain.reshape(-1, 128))
    extra = jnp.broadcast_to(extra[None], (count, size, 128))
    parts = jnp.concatenate([rows.reshape(count, size, -1), extra], axis=2).astype(BF)
    got = lax.all_to_all(parts, "bx", 0, 0, tiled=True)
    total = jnp.sum(got.astype(F32), axis=0)
    gain = total[: gain.shape[1] // 128, rows.shape[1] :].reshape(1, -1)
    mine = total[:, : rows.shape[1]].astype(BF)
    back = lax.all_to_all(jnp.broadcast_to(mine[None], (count,) + mine.shape), "bx", 0, 0, tiled=True)
    return back.reshape(rows.shape), gain


def call(kernel, name, outs, ins, specs, scratch, limit, flops, moved, exps=0, out_specs=None, grid=()):
    return pl.pallas_call(
        kernel,
        out_shape=outs,
        grid=grid,
        in_specs=specs,
        out_specs=jax.tree.map(lambda _: VM, outs) if out_specs is None else out_specs,
        scratch_shapes=scratch,
        compiler_params=pltpu.CompilerParams(vmem_limit_bytes=limit * MIB),
        cost_estimate=pl.CostEstimate(flops=flops, bytes_accessed=moved, transcendentals=exps),
        name=name,
    )(*ins)


def shards(tokens, norm_gain, w_query_key, w_value, w_out, cotangent, block_order,
           neighbour_ids, neighbour_count):
    n, d = tokens.shape[2:]
    extent_x, extent_y, blocks, slots = neighbour_ids.shape
    dims = (extent_x, extent_y, blocks, slots)
    np_ = d // PAIR
    tok, cot = tokens[0, 0], cotangent[0, 0]
    order = block_order[0]
    gain = norm_gain[None, :]
    ids = neighbour_ids.reshape(-1)
    cnt = neighbour_count.reshape(-1)
    pos = jnp.stack([lax.axis_index("bx"), lax.axis_index("by")]).astype(jnp.int32)
    shape = jax.ShapeDtypeStruct

    sends = [shape((2 * BLK, d), BF)] * 4
    sorted_rows, *sent = call(
        functools.partial(sort_kernel, dims), "sort_rows",
        [shape((n, d), BF)] + sends, (pos, ids, cnt, order, tok), [SM, SM, SM, VM, AN],
        [pltpu.VMEM((n, 128), jnp.int32), pltpu.VMEM((n, d), BF), pltpu.SemaphoreType.DMA((1,))], 32, 2 * n * n * d, 4 << 20,
    )
    arrived = [
        step_to(sent[0], "bx", 1), step_to(sent[1], "bx", -1),
        step_to(sent[2], "by", 1), step_to(sent[3], "by", -1),
    ]
    nat, tra = (blocks, np_, BLK, PAIR), (blocks, np_, PAIR, BLK)

    def a_block(dims_):
        return pl.BlockSpec((1,) + dims_[1:], lambda b: (b,) + (0,) * (len(dims_) - 1))

    whole = pl.BlockSpec(memory_space=pltpu.VMEM)
    out_dims = [(n, d), (blocks, d, BLK)] + [nat, tra] * 4
    sc, n_t, *made = call(
        functools.partial(project_kernel, np_), "project", [shape(k, BF) for k in out_dims],
        (order, sorted_rows, cot, gain, w_query_key, w_value, w_out),
        [whole, pl.BlockSpec((BLK, d), lambda b: (b, 0))] + [whole] * 5,
        [pltpu.VMEM((n, 128), jnp.int32)], LIMIT, 2 * n * n * d + 8 * n * d * d, 14 << 20,
        out_specs=[pl.BlockSpec((BLK, d), lambda b: (b, 0))] + [a_block(k) for k in out_dims[1:]], grid=(blocks,),
    )
    pool = blocks + 8
    tile = (slots + 1, BLK, 2 * BLK)
    vmem = pltpu.VMEM
    ins = (pos, ids, cnt, gain, *arrived, w_query_key, w_value, *made, sc, n_t)
    ctx_t, dq_t, own, *back, keep, send, gain_term = call(
        functools.partial(attend_kernel, dims, np_), "attend",
        [shape((d, n), BF)] * 2 + [shape((blocks, 2, np_, BLK, PAIR), F32)]
        + [shape((2, 2, np_, BLK, PAIR), BF)] * 4
        + [shape((n, d), BF), shape((n + 16, d), BF), shape((8, d), F32)],
        ins, [SM] * 3 + [VM] + [AN] * (len(ins) - 4),
        [vmem((4, 2 * BLK, d), BF), vmem((d, 2 * d), BF), vmem((d, d), BF)]
        + [vmem(nat, BF), vmem(tra, BF)] * 2
        + [vmem((pool,) + nat[1:], BF), vmem((pool,) + tra[1:], BF)] * 2
        + [vmem((n, d), BF), vmem((d, pool * BLK), BF)] + [vmem((d, n), BF)] * 2
        + [vmem((pool, 2) + nat[1:], F32)] + [vmem(tile, F32)] * 2 + [vmem(tile, BF)] * 4
        + [vmem((2, n + 16, d), BF), pltpu.SMEM((blocks * slots,), jnp.int32),
           pltpu.SemaphoreType.DMA((20,)), pltpu.SemaphoreType.DMA((13,))],
        LIMIT, 12 * blocks * 5 * BLK * BLK * d, 24 << 20, blocks * 5 * BLK * BLK * 8,
        out_specs=[AN] * 9 + [VM],
    )
    h0, h1, h2, h3 = back
    cores = lax.ppermute(send, "by", [(i, i ^ 1) for i in range(extent_y)])
    b_x = [step_to(h0, "bx", -1), step_to(h1, "bx", 1)]
    mine, *cut, gain_sum = call(
        core_kernel, "add_cores",
        [shape((BLK, d), F32)] + [shape((BLK + 16, d), BF)] * 3 + [shape((8, d), F32)],
        (pos, keep, cores, gain_term), [SM, VM, VM, VM], [], 32, 0, 4 << 20,
    )
    count = extent_y // 2

    def along_y(rows, s):
        return lax.ppermute(rows, "by", [(i, (i + 2 * s) % extent_y) for i in range(extent_y)])

    def other_core(rows):
        return lax.ppermute(rows, "by", [(i, i ^ 1) for i in range(extent_y)])

    got = [along_y(cut[s - 1], s) for s in range(1, count)]
    branch_out, part = call(
        output_kernel, "branch_rows", [shape((n, d), BF), shape((n, d), F32)],
        (order, w_query_key, w_out, ctx_t, dq_t), [VM] * 5, [], 40,
        4 * n * n * d + 4 * n * d * d, 7 << 20,
    )
    got, h2, h3 = lax.optimization_barrier((got, h2, h3))
    b_y = [step_to(h2, "by", -1), step_to(h3, "by", 1)]
    rows, gain_sum = mine, gain_sum[:1]
    for g in got:
        rows = rows + g[:BLK].astype(F32)
        gain_sum = gain_sum + g[BLK : BLK + 1].astype(F32)
    rows, gain_sum, part, branch_out, b_x = lax.optimization_barrier((rows, gain_sum, part, branch_out, b_x))
    rows, gain_sum = across_x(rows, gain_sum)
    rows, part = lax.optimization_barrier((rows, part))
    chunks = [rows] + [along_y(rows, s) for s in range(1, count)]

    grad_rows = call(
        functools.partial(rows_kernel, dims, np_), "token_rows", shape((n, d), F32),
        (pos, ids, cnt, order, tok, gain, w_query_key, w_value, part, own, *b_x, *b_y),
        [SM] * 3 + [VM] * 11,
        [pltpu.VMEM((blocks, 2, np_, BLK, PAIR), F32), pltpu.VMEM((n, 2 * d), BF)],
        56, 4 * n * n * d + 4 * n * d * d, 16 << 20,
    )
    chunks, grad_rows = lax.optimization_barrier((chunks, grad_rows))
    chunks = chunks + [other_core(c) for c in chunks]
    grad_qk, grad_v, grad_o = call(
        place_kernel, "weight_grads", [shape((d, 2 * d), F32), shape((d, d), F32), shape((d, d), F32)],
        (pos, *chunks), [SM] + [VM] * 8, [pltpu.VMEM((4 * d, d), BF)], 32, 0, 6 << 20,
    )
    return (branch_out[None, None], grad_rows[None, None], grad_qk, grad_v, grad_o, gain_sum[0])


def solution(mesh):
    local = P("bx", "by", None, None)
    placed = (local, P(), P(), P(), P(), local, P("bx", "by", None), P(), P())
    return jax.shard_map(
        shards,
        mesh=mesh,
        in_specs=placed,
        out_specs=(local, local, P(), P(), P(), P()),
        check_vma=False,
    )
```

```python
import functools

import jax
import jax.numpy as jnp
from jax import lax
from jax.experimental import pallas as pl
from jax.experimental.pallas import tpu as pltpu
from jax.sharding import PartitionSpec as P

BLK = 256
PAIR = 128
EPSILON = 1e-06
BF = jnp.bfloat16
F32 = jnp.float32
MIB = 1 << 20
LIMIT = 58
WIDE = 512
VM = pl.BlockSpec(memory_space=pltpu.VMEM)
SM = pl.BlockSpec(memory_space=pltpu.SMEM)
AN = pl.BlockSpec(memory_space=pl.ANY)
NT = (((1,), (1,)), ((), ()))


def mm(a, b):
    return jnp.dot(a, b, preferred_element_type=F32)


def mm_nt(a, b):
    return lax.dot_general(a, b, NT, preferred_element_type=F32)


def rms(rows):
    values = rows.astype(F32)
    inv = lax.rsqrt(jnp.mean(values * values, axis=-1, keepdims=True) + EPSILON)
    return values, inv


def named_mask(ids, cnt, reader, owner, blocks, slots):
    mask = jnp.int32(0)
    for b in range(blocks):
        count = cnt[reader * blocks + b]
        for j in range(slots):
            entry = ids[(reader * blocks + b) * slots + j]
            hit = jnp.logical_and(j < count, lax.div(entry, blocks) == owner)
            mask = mask | jnp.where(hit, jnp.left_shift(1, lax.rem(entry, blocks)), 0)
    return mask


def first_two(mask, blocks):
    def lowest(m):
        at = jnp.int32(blocks - 1)
        for b in range(blocks - 2, -1, -1):
            at = jnp.where((m & (1 << b)) != 0, b, at)
        return at

    first = lowest(mask)
    return first, lowest(mask & ~jnp.left_shift(1, first))


def send_table(ids, cnt, pos, extent_x, extent_y, blocks, slots):
    x, y = pos[0], pos[1]
    me = x * extent_y + y
    readers = (
        jnp.minimum(x + 1, extent_x - 1) * extent_y + y,
        jnp.maximum(x - 1, 0) * extent_y + y,
        x * extent_y + jnp.minimum(y + 1, extent_y - 1),
        x * extent_y + jnp.maximum(y - 1, 0),
    )
    return [first_two(named_mask(ids, cnt, r, me, blocks, slots), blocks) for r in readers]


def pool_table(ids, cnt, pos, extent_y, blocks, slots):
    me = pos[0] * extent_y + pos[1]
    owners = (me - extent_y, me + extent_y, me - 1, me + 1)
    masks = [named_mask(ids, cnt, me, o, blocks, slots) for o in owners]
    table = []
    for b in range(blocks):
        row = []
        for j in range(slots):
            entry = ids[(me * blocks + b) * slots + j]
            owner, off = lax.div(entry, blocks), lax.rem(entry, blocks)
            at = off
            for seg, (o, mask) in enumerate(zip(owners, masks)):
                below = mask & (jnp.left_shift(1, off) - 1)
                at = jnp.where(owner == o, blocks + 2 * seg + jnp.where(below != 0, 1, 0), at)
            live = j < cnt[me * blocks + b]
            row.append((jnp.where(live, at, b), live))
        table.append(row)
    return table


def order_columns(order_ref):
    n = order_ref.shape[1]
    return jnp.broadcast_to(order_ref[...], (128, n)).T


def one_hot_rows(cols, n):
    lane = lax.broadcasted_iota(jnp.int32, cols.shape, 1)
    return jnp.concatenate(
        [(cols == lane + c).astype(F32).astype(BF) for c in range(0, n, 128)], axis=1
    )


def one_hot_back(order_ref, start, rows):
    n = order_ref.shape[1]
    row = lax.broadcasted_iota(jnp.int32, (rows, n), 0) + start
    return (row == order_ref[...]).astype(F32).astype(BF)


def sort_kernel(dims, pos, ids, cnt, order, tok_in, out, s0, s1, s2, s3, cols, tok, sem):
    extent_x, extent_y, blocks, slots = dims
    n = tok.shape[0]
    copy = pltpu.make_async_copy(tok_in, tok, sem.at[0])
    copy.start()
    cols[...] = order_columns(order)
    table = send_table(ids, cnt, pos, extent_x, extent_y, blocks, slots)
    copy.wait()

    def body(b, _):
        rows = pl.ds(pl.multiple_of(b * BLK, BLK), BLK)
        out[rows, :] = mm(one_hot_rows(cols[rows, :], n), tok[...]).astype(BF)
        return 0

    lax.fori_loop(0, n // BLK, body, 0)
    for ref, pair in zip((s0, s1, s2, s3), table):
        for k, b in enumerate(pair):
            ref[k * BLK : (k + 1) * BLK, :] = out[pl.ds(pl.multiple_of(b * BLK, BLK), BLK), :]


def project_kernel(np_, order, tok, cot, gain, w_qk, w_v, w_out, sc, n_t, *rest):
    *outs, cols = rest
    n, d = cot.shape
    b = pl.program_id(0)

    @pl.when(b == 0)
    def _():
        cols[...] = order_columns(order)

    rows = pl.ds(pl.multiple_of(b * BLK, BLK), BLK)
    grad = mm(one_hot_rows(cols[rows, :], n), cot[...]).astype(BF)
    sc[...] = grad
    values, inv = rms(tok[...])
    normed = (values * inv * gain[...]).astype(BF)
    n_t[0] = normed.T
    query = (mm(normed, w_qk[:, :d]).astype(BF)) * BF(0.125)
    key = mm(normed, w_qk[:, d:]).astype(BF)
    value = mm(normed, w_v[...]).astype(BF)
    dctx = mm_nt(grad, w_out[...]).astype(BF)
    for at, mat in enumerate((query, key, value, dctx)):
        mat_t = mat.T
        for p in range(np_):
            outs[2 * at][0, p] = mat[:, p * PAIR : (p + 1) * PAIR]
            outs[2 * at + 1][0, p] = mat_t[p * PAIR : (p + 1) * PAIR, :]


def attend_kernel(dims, np_, pos, ids, cnt, gain, r0, r1, r2, r3, w_qk_in, w_v_in,
                  qn_in, qt_in, kn_in, kt_in, vn_in, vt_in, gn_in, gt_in, sc_in, nt_in,
                  ctx_out, dq_out, own, h0, h1, h2, h3, keep, send, gain_out,
                  far, w_qk, w_v, qn, qt, gn, gt, pkn, pkt, pvn, pvt, sc, n_t, ctx_t, dq_t, acc,
                  s_scr, dp_scr, p_a, ds_a, p_b, ds_b, terms, where_ref, sem_in, sem_out):
    extent_x, extent_y, blocks, slots = dims
    d = w_v.shape[0]
    mine = pl.ds(0, blocks)
    scratch = ((p_a, ds_a), (p_b, ds_b))
    first, later = [], []

    def fetch(src, dst, into):
        copy = pltpu.make_async_copy(src, dst, sem_in.at[len(first) + len(later)])
        copy.start()
        into.append(copy)

    fetch(w_qk_in, w_qk, first)
    fetch(w_v_in, w_v, first)
    for seg, ref in enumerate((r0, r1, r2, r3)):
        fetch(ref, far.at[seg], first)
    for src, dst in ((kn_in, pkn.at[mine]), (kt_in, pkt.at[mine]), (vn_in, pvn.at[mine]),
                     (vt_in, pvt.at[mine]), (qt_in, qt), (gt_in, gt), (qn_in, qn), (gn_in, gn),
                     (sc_in, sc)):
        fetch(src, dst, later)
    for b in range(blocks):
        fetch(nt_in.at[b], n_t.at[:, pl.ds(b * BLK, BLK)], later)
    table = pool_table(ids, cnt, pos, extent_y, blocks, slots)
    for b in range(blocks):
        for j in range(slots):
            where_ref[b * slots + j] = table[b][j][0]
    acc[...] = jnp.zeros_like(acc)
    for copy in first:
        copy.wait()

    def remote(i, _):
        rows = pl.ds(pl.multiple_of(lax.rem(i, 2) * BLK, BLK), BLK)
        values, inv = rms(far[lax.div(i, 2), rows, :])
        normed = (values * inv * gain[...]).astype(BF)
        n_t[:, pl.ds(pl.multiple_of((blocks + i) * BLK, BLK), BLK)] = normed.T
        made = mm(normed, w_qk[:, d:]).astype(BF)
        made_v = mm(normed, w_v[...]).astype(BF)
        for mat, nat, tra in ((made, pkn, pkt), (made_v, pvn, pvt)):
            mat_t = mat.T
            for p in range(np_):
                nat[blocks + i, p] = mat[:, p * PAIR : (p + 1) * PAIR]
                tra[blocks + i, p] = mat_t[p * PAIR : (p + 1) * PAIR, :]
        return 0

    lax.fori_loop(0, 8, remote, 0, unroll=2)
    for copy in later:
        copy.wait()
    lane = lax.broadcasted_iota(jnp.int32, (1, PAIR), 1)
    low_lanes = (lane < PAIR // 2).astype(F32).astype(BF)
    high_lanes = (lane >= PAIR // 2).astype(F32).astype(BF)
    half = PAIR // 2

    def diagonal(mat):
        zero = jnp.zeros((half, BLK), BF)
        return jnp.concatenate(
            [jnp.concatenate([mat[:half], zero], axis=1), jnp.concatenate([zero, mat[half:]], axis=1)],
            axis=0,
        )

    def weigh(b, p, at, p_scr, ds_scr):
        q_diag, g_diag = diagonal(qt[b, p]), diagonal(gt[b, p])
        top = None
        for j, k in enumerate(at):
            s = mm(pkn[k, p], q_diag)
            s_scr[j] = s
            m = jnp.max(s, axis=0, keepdims=True)
            top = m if top is None else jnp.maximum(top, m)
        total = jnp.zeros((1, 2 * BLK), F32)
        centre = jnp.zeros((1, 2 * BLK), F32)
        for j, k in enumerate(at):
            e = jnp.exp(s_scr[j] - top)
            s_scr[j] = e
            total += jnp.sum(e, axis=0, keepdims=True)
            dp = mm(pvn[k, p], g_diag)
            dp_scr[j] = dp
            centre += jnp.sum(e * dp, axis=0, keepdims=True)
        scale = 1.0 / total
        centre = centre * scale
        for j in range(len(at)):
            prob = s_scr[j] * scale
            p_scr[j] = prob.astype(BF)
            ds_scr[j] = (prob * (dp_scr[j] - centre)).astype(BF)

    def spread(b, p, at, p_scr, ds_scr):
        q_rows = qn[b, p]
        g_rows = gn[b, p]
        q_mask = jnp.concatenate([q_rows * low_lanes, q_rows * high_lanes], axis=0)
        g_mask = jnp.concatenate([g_rows * low_lanes, g_rows * high_lanes], axis=0)
        for h in range(2):
            feats, lanes = slice(h * half, (h + 1) * half), slice(h * BLK, (h + 1) * BLK)
            ctx = dq = None
            for j, k in enumerate(at):
                c = mm(pvt[k, p, feats, :], p_scr[j, :, lanes])
                t = mm(pkt[k, p, feats, :], ds_scr[j, :, lanes])
                ctx = c if ctx is None else ctx + c
                dq = t if dq is None else dq + t
            rows = pl.ds(pl.multiple_of(p * PAIR + h * half, half), half)
            cols = pl.ds(pl.multiple_of(b * BLK, BLK), BLK)
            ctx_t[rows, cols] = ctx.astype(BF)
            dq_t[rows, cols] = (dq * 0.125).astype(BF)
        for j, k in enumerate(at):
            acc[k, 0, p] += mm(ds_scr[j], q_mask)
            acc[k, 1, p] += mm(p_scr[j], g_mask)

    me = pos[0] * extent_y + pos[1]

    def block(b, _):
        count = cnt[me * blocks + b]
        for live in range(1, slots + 1):

            @pl.when(count == live)
            def _():
                at = [b] + [where_ref[b * slots + j] for j in range(live)]

                def two(i, c):
                    for k, scr in enumerate(scratch):
                        weigh(b, 2 * i + k, at, *scr)
                    for k, scr in enumerate(scratch):
                        spread(b, 2 * i + k, at, *scr)
                    return c

                lax.fori_loop(0, np_ // 2, two, 0)

        return 0

    lax.fori_loop(0, blocks, block, 0)
    out = []

    def ship(src, dst):
        copy = pltpu.make_async_copy(src, dst, sem_out.at[len(out)])
        copy.start()
        out.append(copy)

    ship(ctx_t, ctx_out)
    ship(dq_t, dq_out)
    ship(acc.at[mine], own)

    def lower(b, _):
        for p in range(np_):
            pkn[b, p] = acc[b, 0, p].astype(BF)
            pvn[b, p] = acc[b, 1, p].astype(BF)
        return 0

    lax.fori_loop(0, blocks + 8, lower, 0)
    for seg, ref in enumerate((h0, h1, h2, h3)):
        part = pl.ds(blocks + 2 * seg, 2)
        ship(pkn.at[part], ref.at[0])
        ship(pvn.at[part], ref.at[1])
    core = lax.rem(pos[1], 2)
    total = jnp.zeros((d, 1), F32)

    def place(i, value):
        terms[lax.rem(i + core, 2), (i // 2) * BLK : (i // 2 + 1) * BLK, :] = value.astype(BF)

    g_q = mm_nt(n_t[:, : blocks * BLK], dq_t[...])
    g_o = mm(ctx_t[...], sc[...])
    for i, g in ((0, g_q), (6, g_o)):
        place(i, g[:BLK])
        place(i + 1, g[BLK:])
    total += jnp.sum(g_q * w_qk[:, :d].astype(F32), axis=1, keepdims=True)
    for i, pool, w, lo in ((2, pkn, w_qk, d), (4, pvn, w_v, 0)):
        made = []
        for p in range(0, np_, 2):
            cols = [jnp.concatenate([pool[b, p], pool[b, p + 1]], axis=1) for b in range(blocks + 8)]
            g = mm(n_t[...], jnp.concatenate(cols, axis=0))
            at = lo + p * PAIR
            total += jnp.sum(g * w[:, at : at + 2 * PAIR].astype(F32), axis=1, keepdims=True)
            made.append(g)
        g = jnp.concatenate(made, axis=1)
        place(i, g[:BLK])
        place(i + 1, g[BLK:])
    gain_term = jnp.broadcast_to(total, (d, 128)).T[:8] / gain[...]
    gain_out[...] = gain_term
    terms[:, blocks * BLK :, :] = jnp.broadcast_to(gain_term[:1].astype(BF)[None], (2, 16, d))
    ship(terms.at[0, pl.ds(0, blocks * BLK)], keep)
    ship(terms.at[1], send)
    for copy in out:
        copy.wait()


def core_kernel(pos, keep, got, gain, own, s1, s2, s3, gain_out):
    size, d = own.shape
    rows = 4 * size
    total = gain[:1] + got[rows : rows + 1, :].astype(F32)
    gain_out[...] = jnp.broadcast_to(total, gain_out.shape)
    y = lax.div(pos[1], 2)
    for s, ref in enumerate((own, s1, s2, s3)):
        at = pl.ds(pl.multiple_of(lax.rem(y + s, 4) * size, size), size)
        value = keep[at, :].astype(F32) + got[at, :].astype(F32)
        if s:
            ref[:size, :] = value.astype(BF)
            ref[size:, :] = jnp.broadcast_to(total, (ref.shape[0] - size, d)).astype(BF)
        else:
            ref[...] = value


def output_kernel(order, w_qk, w_out, ctx_t, dq_t, out, part):
    d = w_out.shape[0]

    def body(a, _):
        rows = pl.ds(pl.multiple_of(a * WIDE, WIDE), WIDE)
        back = one_hot_back(order, a * WIDE, WIDE)
        ctx = mm_nt(back, ctx_t[...]).astype(BF)
        dq = mm_nt(back, dq_t[...]).astype(BF)
        out[rows, :] = mm(ctx, w_out[...]).astype(BF)
        part[rows, :] = mm_nt(dq, w_qk[:, :d])
        return 0

    lax.fori_loop(0, out.shape[0] // WIDE, body, 0)


def rows_kernel(dims, np_, pos, ids, cnt, order, tok, gain, w_qk, w_v, part, own, b0, b1, b2, b3,
                out, acc, rows_scr):
    extent_x, extent_y, blocks, slots = dims
    d = w_v.shape[0]
    acc[...] = own[...]
    table = send_table(ids, cnt, pos, extent_x, extent_y, blocks, slots)
    for ref, pair in zip((b0, b1, b2, b3), table):
        for k, b in enumerate(pair):
            acc[b, 0] += ref[0, k].astype(F32)
            acc[b, 1] += ref[1, k].astype(F32)
    for half in range(2):
        for p in range(np_):
            lo = half * d + p * PAIR
            for b in range(blocks):
                rows_scr[b * BLK : (b + 1) * BLK, lo : lo + PAIR] = acc[b, half, p].astype(BF)

    def body(a, _):
        rows = pl.ds(pl.multiple_of(a * WIDE, WIDE), WIDE)
        back = one_hot_back(order, a * WIDE, WIDE)
        mine = mm(back, rows_scr[...]).astype(BF)
        grad = part[rows, :] + mm_nt(mine[:, :d], w_qk[:, d:]) + mm_nt(mine[:, d:], w_v[...])
        values, inv = rms(tok[rows, :])
        u = grad * gain[...]
        mean = jnp.mean(values * u, axis=-1, keepdims=True)
        out[rows, :] = inv * u - values * (inv * inv * inv * mean)
        return 0

    lax.fori_loop(0, out.shape[0] // WIDE, body, 0)


def place_kernel(pos, *refs):
    *parts, qk, v, o, rows = refs
    d = v.shape[0]
    count = len(parts) // 2
    core, y = lax.rem(pos[1], 2), lax.div(pos[1], 2)
    size = parts[0].shape[0]
    for i, ref in enumerate(parts):
        c = core if i < count else 1 - core
        at = (lax.rem(y - i % count + count, count) * 2 + c) * size
        rows[pl.ds(pl.multiple_of(at, size), size), :] = ref[...]
    qk[:, :d] = rows[:d, :].astype(F32)
    qk[:, d:] = rows[d : 2 * d, :].astype(F32)
    v[...] = rows[2 * d : 3 * d, :].astype(F32)
    o[...] = rows[3 * d :, :].astype(F32)


def step_to(block, axis, distance):
    n = lax.axis_size(axis)
    route = [(i, i + distance) for i in range(n) if 0 <= i + distance < n]
    return lax.ppermute(block, axis, route)


def across_x(rows, gain):
    count = lax.axis_size("bx")
    size = rows.shape[0] // count
    extra = jnp.zeros((size, 128), F32).at[: gain.shape[1] // 128].set(gain.reshape(-1, 128))
    extra = jnp.broadcast_to(extra[None], (count, size, 128))
    parts = jnp.concatenate([rows.reshape(count, size, -1), extra], axis=2).astype(BF)
    got = lax.all_to_all(parts, "bx", 0, 0, tiled=True)
    total = jnp.sum(got.astype(F32), axis=0)
    gain = total[: gain.shape[1] // 128, rows.shape[1] :].reshape(1, -1)
    mine = total[:, : rows.shape[1]].astype(BF)
    back = lax.all_to_all(jnp.broadcast_to(mine[None], (count,) + mine.shape), "bx", 0, 0, tiled=True)
    return back.reshape(rows.shape), gain


def call(kernel, name, outs, ins, specs, scratch, limit, flops, moved, exps=0, out_specs=None, grid=()):
    return pl.pallas_call(
        kernel,
        out_shape=outs,
        grid=grid,
        in_specs=specs,
        out_specs=jax.tree.map(lambda _: VM, outs) if out_specs is None else out_specs,
        scratch_shapes=scratch,
        compiler_params=pltpu.CompilerParams(vmem_limit_bytes=limit * MIB),
        cost_estimate=pl.CostEstimate(flops=flops, bytes_accessed=moved, transcendentals=exps),
        name=name,
    )(*ins)


def shards(tokens, norm_gain, w_query_key, w_value, w_out, cotangent, block_order,
           neighbour_ids, neighbour_count):
    n, d = tokens.shape[2:]
    extent_x, extent_y, blocks, slots = neighbour_ids.shape
    dims = (extent_x, extent_y, blocks, slots)
    np_ = d // PAIR
    tok, cot = tokens[0, 0], cotangent[0, 0]
    order = block_order[0]
    gain = norm_gain[None, :]
    ids = neighbour_ids.reshape(-1)
    cnt = neighbour_count.reshape(-1)
    pos = jnp.stack([lax.axis_index("bx"), lax.axis_index("by")]).astype(jnp.int32)
    shape = jax.ShapeDtypeStruct

    sends = [shape((2 * BLK, d), BF)] * 4
    sorted_rows, *sent = call(
        functools.partial(sort_kernel, dims), "sort_rows",
        [shape((n, d), BF)] + sends, (pos, ids, cnt, order, tok), [SM, SM, SM, VM, AN],
        [pltpu.VMEM((n, 128), jnp.int32), pltpu.VMEM((n, d), BF), pltpu.SemaphoreType.DMA((1,))], 32, 2 * n * n * d, 4 << 20,
    )
    arrived = [
        step_to(sent[0], "bx", 1), step_to(sent[1], "bx", -1),
        step_to(sent[2], "by", 1), step_to(sent[3], "by", -1),
    ]
    nat, tra = (blocks, np_, BLK, PAIR), (blocks, np_, PAIR, BLK)

    def a_block(dims_):
        return pl.BlockSpec((1,) + dims_[1:], lambda b: (b,) + (0,) * (len(dims_) - 1))

    whole = pl.BlockSpec(memory_space=pltpu.VMEM)
    out_dims = [(n, d), (blocks, d, BLK)] + [nat, tra] * 4
    sc, n_t, *made = call(
        functools.partial(project_kernel, np_), "project", [shape(k, BF) for k in out_dims],
        (order, sorted_rows, cot, gain, w_query_key, w_value, w_out),
        [whole, pl.BlockSpec((BLK, d), lambda b: (b, 0))] + [whole] * 5,
        [pltpu.VMEM((n, 128), jnp.int32)], LIMIT, 2 * n * n * d + 8 * n * d * d, 14 << 20,
        out_specs=[pl.BlockSpec((BLK, d), lambda b: (b, 0))] + [a_block(k) for k in out_dims[1:]], grid=(blocks,),
    )
    pool = blocks + 8
    tile = (slots + 1, BLK, 2 * BLK)
    vmem = pltpu.VMEM
    ins = (pos, ids, cnt, gain, *arrived, w_query_key, w_value, *made, sc, n_t)
    ctx_t, dq_t, own, *back, keep, send, gain_term = call(
        functools.partial(attend_kernel, dims, np_), "attend",
        [shape((d, n), BF)] * 2 + [shape((blocks, 2, np_, BLK, PAIR), F32)]
        + [shape((2, 2, np_, BLK, PAIR), BF)] * 4
        + [shape((n, d), BF), shape((n + 16, d), BF), shape((8, d), F32)],
        ins, [SM] * 3 + [VM] + [AN] * (len(ins) - 4),
        [vmem((4, 2 * BLK, d), BF), vmem((d, 2 * d), BF), vmem((d, d), BF)]
        + [vmem(nat, BF), vmem(tra, BF)] * 2
        + [vmem((pool,) + nat[1:], BF), vmem((pool,) + tra[1:], BF)] * 2
        + [vmem((n, d), BF), vmem((d, pool * BLK), BF)] + [vmem((d, n), BF)] * 2
        + [vmem((pool, 2) + nat[1:], F32)] + [vmem(tile, F32)] * 2 + [vmem(tile, BF)] * 4
        + [vmem((2, n + 16, d), BF), pltpu.SMEM((blocks * slots,), jnp.int32),
           pltpu.SemaphoreType.DMA((20,)), pltpu.SemaphoreType.DMA((13,))],
        LIMIT, 12 * blocks * 5 * BLK * BLK * d, 24 << 20, blocks * 5 * BLK * BLK * 8,
        out_specs=[AN] * 9 + [VM],
    )
    h0, h1, h2, h3 = back
    cores = lax.ppermute(send, "by", [(i, i ^ 1) for i in range(extent_y)])
    b_x = [step_to(h0, "bx", -1), step_to(h1, "bx", 1)]
    mine, *cut, gain_sum = call(
        core_kernel, "add_cores",
        [shape((BLK, d), F32)] + [shape((BLK + 16, d), BF)] * 3 + [shape((8, d), F32)],
        (pos, keep, cores, gain_term), [SM, VM, VM, VM], [], 32, 0, 4 << 20,
    )
    count = extent_y // 2

    def along_y(rows, s):
        return lax.ppermute(rows, "by", [(i, (i + 2 * s) % extent_y) for i in range(extent_y)])

    def other_core(rows):
        return lax.ppermute(rows, "by", [(i, i ^ 1) for i in range(extent_y)])

    got = [along_y(cut[s - 1], s) for s in range(1, count)]
    branch_out, part = call(
        output_kernel, "branch_rows", [shape((n, d), BF), shape((n, d), F32)],
        (order, w_query_key, w_out, ctx_t, dq_t), [VM] * 5, [], 24,
        4 * n * n * d + 4 * n * d * d, 7 << 20,
    )
    got, h2, h3 = lax.optimization_barrier((got, h2, h3))
    b_y = [step_to(h2, "by", -1), step_to(h3, "by", 1)]
    rows, gain_sum = mine, gain_sum[:1]
    for g in got:
        rows = rows + g[:BLK].astype(F32)
        gain_sum = gain_sum + g[BLK : BLK + 1].astype(F32)
    rows, gain_sum, part, branch_out, b_x = lax.optimization_barrier((rows, gain_sum, part, branch_out, b_x))
    rows, gain_sum = across_x(rows, gain_sum)
    rows, part = lax.optimization_barrier((rows, part))
    chunks = [rows] + [along_y(rows, s) for s in range(1, count)]

    grad_rows = call(
        functools.partial(rows_kernel, dims, np_), "token_rows", shape((n, d), F32),
        (pos, ids, cnt, order, tok, gain, w_query_key, w_value, part, own, *b_x, *b_y),
        [SM] * 3 + [VM] * 11,
        [pltpu.VMEM((blocks, 2, np_, BLK, PAIR), F32), pltpu.VMEM((n, 2 * d), BF)],
        30, 4 * n * n * d + 4 * n * d * d, 16 << 20,
    )
    chunks, grad_rows = lax.optimization_barrier((chunks, grad_rows))
    chunks = chunks + [other_core(c) for c in chunks]
    grad_qk, grad_v, grad_o = call(
        place_kernel, "weight_grads", [shape((d, 2 * d), F32), shape((d, d), F32), shape((d, d), F32)],
        (pos, *chunks), [SM] + [VM] * 8, [pltpu.VMEM((4 * d, d), BF)], 32, 0, 6 << 20,
    )
    return (branch_out[None, None], grad_rows[None, None], grad_qk, grad_v, grad_o, gain_sum[0])


def solution(mesh):
    local = P("bx", "by", None, None)
    placed = (local, P(), P(), P(), P(), local, P("bx", "by", None), P(), P())
    return jax.shard_map(
        shards,
        mesh=mesh,
        in_specs=placed,
        out_specs=(local, local, P(), P(), P(), P()),
        check_vma=False,
    )
```
